256 devices in a mesh: tm: 32 (over x, y, core), coef: 8 (over z).
Axes of the slice: x: 4, y: 4, z: 8, core: 2. Of those that a mesh axis runs over, the one named last changes fastest.
Arguments:
- design_lith: bfloat16 [34816, 32768], P('coef', 'tm'), may hold values from -0.03125 to 0.03125
- design_core: bfloat16 [440, 32768], P('coef', 'tm'), may hold values from -0.25 to 0.25
- sample_phase: float32 [32768], P('tm'), may hold values from 0 to 1
- data_weight: float32 [32768], P('tm'), may hold values from 0.1 to 1
- counts: int32 [256], P('tm'), may hold values from 1 to 128, as said below
- knot_index: int32 [256], P('tm'), may hold values from 0 to 255, as said below
- lith_damping: float32 [34816], P('coef'), may hold values from 0.3 to 3
- core_damping: float32 [440], P('coef'), may hold values from 0.3 to 3
- lith_solution: float32 [64, 34816], P(None, 'coef'), may hold values from -6 to 6
- lith_residual: float32 [64, 34816], P(None, 'coef'), may hold values from -6 to 6
- lith_direction: float32 [64, 34816], P(None, 'coef'), may hold values from -6 to 6
- core_solution: float32 [64, 440, 256], P(None, 'coef', 'tm'), may hold values from -6 to 6
- core_residual: float32 [64, 440, 256], P(None, 'coef', 'tm'), may hold values from -6 to 6
- core_direction: float32 [64, 440, 256], P(None, 'coef', 'tm'), may hold values from -6 to 6
Outputs:
- new_lith_solution: float32 [64, 34816], P(None, 'coef')
- new_lith_residual: float32 [64, 34816], P(None, 'coef')
- new_lith_direction: float32 [64, 34816], P(None, 'coef')
- new_core_solution: float32 [64, 440, 256], P(None, 'coef', 'tm')
- new_core_residual: float32 [64, 440, 256], P(None, 'coef', 'tm')
- new_core_direction: float32 [64, 440, 256], P(None, 'coef', 'tm')
The draws below stay inside these ranges and needn't reach their ends.
Inputs may be any that keep to these rules, and one draw needn't show every extreme that they name: `counts`: quiet samples of a segment occupy its first slots; the rest are padding; some segment is full; the last segment of each index of tm holds at least 32 quiet samples. `knot_index`: segment g lies in a knot interval from (g // 8) * 8 to that plus 8 - 1; the first segment lies in the first interval, and the last segment of each index of tm in the last interval of its range.
All inputs are finite; a program needn't handle non-finite values.
Results may differ from the reference program's by a relative error of at most 0.0003.
Values sent between devices are 32-bit elements; how exact they have to be, the bound alone decides.
No kernel may reach another device: no remote copies, remote signals or barrier semaphores. Data moves between devices by JAX's collectives and lax.ppermute only.
A program may use at most 64 MiB of HBM per device.

```python
import math
import jax
import jax.numpy as jnp
from jax import lax

NL = 34816
NC = 440
MEMBERS = 64
SEG_ROWS = 128
SEG_DEV = 8
S_DEV = 8
SEGMENTS = 256
SAMPLES = 32768
SPLINES = 256


def draw_counts(key, part):
    key = jax.random.fold_in(key, 11)
    key_ceiling, key_drawn, key_full = jax.random.split(key, 3)
    groups = SEGMENTS // SEG_DEV
    ceiling = jax.random.randint(key_ceiling, (groups, 1), SEG_ROWS // 4, SEG_ROWS + 1)
    drawn_counts = jax.random.randint(key_drawn, (groups, SEG_DEV), 1, SEG_ROWS + 1)
    counts = jnp.minimum(drawn_counts, ceiling)
    last_column = jnp.arange(SEG_DEV, dtype=jnp.int32)[None, :] == SEG_DEV - 1
    counts = jnp.where(last_column, ceiling, counts).reshape(SEGMENTS)
    full_segment = jax.random.randint(key_full, (), 0, SEGMENTS)
    return counts.at[full_segment].set(SEG_ROWS).astype(jnp.int32)


def draw_knot_index(key, part):
    key = jax.random.fold_in(key, 23)
    segment = jnp.arange(SEGMENTS, dtype=jnp.int32)
    device_group = segment // SEG_DEV
    offsets = jax.random.randint(key, (SEGMENTS,), 0, S_DEV)
    offsets = jnp.where(segment % SEG_DEV == SEG_DEV - 1, S_DEV - 1, offsets)
    offsets = jnp.where(segment == 0, 0, offsets)
    return (device_group * S_DEV + offsets).astype(jnp.int32)


def level_of(key, extent, shards, smallest, largest):
    gain, own = 1.0, jax.random.fold_in(key, 6)
    for position, parts in shards:
        heights = jnp.exp(jax.random.uniform(jax.random.fold_in(own, position), (parts,), jnp.float32, smallest / len(shards), largest / len(shards)))
        gain = gain * jnp.repeat(heights, extent[position] // parts).reshape([-1 if axis == position else 1 for axis in range(len(extent))])
    return gain


def centred(own_key, extent, scale, reach, shards=(), held_as=jnp.bfloat16):
    array = jax.random.normal(own_key, extent, jnp.float32) * scale
    if len(shards) > 0:
        array = level_of(own_key, extent, shards, -0.22, 0.18) * array
    return jnp.clip(array, min=-reach, max=reach).astype(held_as)


def setup_inputs(seed: int = 0) -> dict:
    arg_keys = jax.random.split(jax.random.key(seed), 15)
    return {
        "design_lith": centred(arg_keys[0], (NL, SAMPLES), NL ** -0.5, 0.03125, ((0, 8), (1, 32))),
        "design_core": centred(arg_keys[1], (NC, SAMPLES), NC ** -0.5, 0.25, ((0, 8), (1, 32))),
        "sample_phase": jnp.clip(1.0 * jax.random.uniform(arg_keys[2], (SAMPLES,), jnp.float32) ** level_of(arg_keys[2], (SAMPLES,), ((0, 32),), -0.2, 0.2), 0.0, 1.0),
        "data_weight": jnp.clip(jnp.exp(math.log(1.0) - 2.3025851 * jax.random.uniform(arg_keys[3], (SAMPLES,), jnp.float32) ** level_of(arg_keys[3], (SAMPLES,), ((0, 32),), -0.2, 0.2)), 0.1, 1.0),
        "counts": draw_counts(jax.random.fold_in(arg_keys[14], 71), 0),
        "knot_index": draw_knot_index(jax.random.fold_in(arg_keys[14], 71), 0),
        "lith_damping": jnp.clip(jnp.exp(math.log(3.0) - 2.3025851 * jax.random.uniform(arg_keys[6], (NL,), jnp.float32) ** level_of(arg_keys[6], (NL,), ((0, 8),), -0.2, 0.2)), 0.3, 3.0),
        "core_damping": jnp.clip(jnp.exp(math.log(3.0) - 2.3025851 * jax.random.uniform(arg_keys[7], (NC,), jnp.float32) ** level_of(arg_keys[7], (NC,), ((0, 8),), -0.2, 0.2)), 0.3, 3.0),
        "lith_solution": centred(arg_keys[8], (MEMBERS, NL), 1.0, 6.0, ((1, 8),), jnp.float32),
        "lith_residual": centred(arg_keys[9], (MEMBERS, NL), 1.0, 6.0, ((1, 8),), jnp.float32),
        "lith_direction": centred(arg_keys[10], (MEMBERS, NL), 1.0, 6.0, ((1, 8),), jnp.float32),
        "core_solution": centred(arg_keys[11], (MEMBERS, NC, SPLINES), 1.0, 6.0, ((1, 8), (2, 32)), jnp.float32),
        "core_residual": centred(arg_keys[12], (MEMBERS, NC, SPLINES), 1.0, 6.0, ((1, 8), (2, 32)), jnp.float32),
        "core_direction": centred(arg_keys[13], (MEMBERS, NC, SPLINES), 1.0, 6.0, ((1, 8), (2, 32)), jnp.float32),
    }


def spline_values(fraction):
    basis_now = [jnp.ones_like(fraction)]
    for degree in range(1, 6):
        basis_next = []
        for s in range(degree + 1):
            lower_term = basis_now[s - 1] if s >= 1 else jnp.zeros_like(fraction)
            upper_term = basis_now[s] if s < degree else jnp.zeros_like(fraction)
            basis_next.append(((fraction + (degree - s)) * lower_term + ((s + 1) - fraction) * upper_term) / degree)
        basis_now = basis_next
    return jnp.stack(basis_now)


def split_two(values):
    high_part = lax.optimization_barrier(values.astype(jnp.bfloat16))
    low_part = (values - high_part.astype(jnp.float32)).astype(jnp.bfloat16)
    return jnp.concatenate([high_part, low_part], axis=0)


def reference(design_lith, design_core, sample_phase, data_weight, counts, knot_index, lith_damping, core_damping, lith_solution, lith_residual, lith_direction, core_solution, core_residual, core_direction):
    members = lith_direction.shape[0]
    highest = lax.Precision.HIGHEST
    spline_basis = spline_values(sample_phase)
    positions = jnp.arange(SAMPLES, dtype=jnp.int32)
    live_mask = (positions % SEG_ROWS < jnp.repeat(counts, SEG_ROWS)).astype(jnp.float32)
    weight = data_weight * live_mask
    lith_terms = jnp.dot(split_two(lith_direction), design_lith, preferred_element_type=jnp.float32)
    lith_pred = lith_terms[:members] + lith_terms[members:]
    extended = jnp.pad(core_direction, ((0, 0), (0, 0), (0, 5)))
    segment_ids = jnp.arange(SEGMENTS, dtype=jnp.int32)

    def core_block(segment):
        first_row = segment * SEG_ROWS
        local_basis = lax.dynamic_slice_in_dim(spline_basis, first_row, SEG_ROWS, 1)
        local_design = lax.dynamic_slice_in_dim(design_core, first_row, SEG_ROWS, 1).astype(jnp.float32)
        coefficients = lax.dynamic_slice_in_dim(extended, knot_index[segment], 6, 2)
        combined = jnp.einsum("vjs,si->vji", coefficients, local_basis, precision=highest)
        return jnp.sum(combined * local_design[None], axis=1)

    core_pred = lax.map(core_block, segment_ids)
    core_pred = jnp.transpose(core_pred, (1, 0, 2)).reshape(members, SAMPLES)
    residual = weight[None] * (lith_pred + core_pred)
    grad_terms = lax.dot_general(split_two(residual), design_lith, (((1,), (1,)), ((), ())), preferred_element_type=jnp.float32)
    lith_grad = grad_terms[:members] + grad_terms[members:]

    def add_segment(grad_total, segment):
        first_row = segment * SEG_ROWS
        local_basis = lax.dynamic_slice_in_dim(spline_basis, first_row, SEG_ROWS, 1)
        local_design = lax.dynamic_slice_in_dim(design_core, first_row, SEG_ROWS, 1).astype(jnp.float32)
        local_residual = lax.dynamic_slice_in_dim(residual, first_row, SEG_ROWS, 1)
        weighted = local_residual[:, None, :] * local_design[None]
        contribution = jnp.einsum("vji,si->vjs", weighted, local_basis, precision=highest)
        start_col = knot_index[segment]
        current = lax.dynamic_slice_in_dim(grad_total, start_col, 6, 2)
        return lax.dynamic_update_slice_in_dim(grad_total, current + contribution, start_col, 2), None

    grad_start = jnp.zeros((members, NC, SPLINES + 5), jnp.float32)
    grad_total, unused = lax.scan(add_segment, grad_start, segment_ids)
    core_grad = grad_total[:, :, :SPLINES]
    lith_image = lith_grad + lith_damping[None] * lith_direction
    core_image = core_grad + core_damping[None, :, None] * core_direction
    norm_before = jnp.sum(lith_residual * lith_residual, axis=1) + jnp.sum(core_residual * core_residual, axis=(1, 2))
    curvature = jnp.sum(lith_direction * lith_image, axis=1) + jnp.sum(core_direction * core_image, axis=(1, 2))
    step_size = norm_before / curvature
    new_lith_solution = lith_solution + step_size[:, None] * lith_direction
    new_core_solution = core_solution + step_size[:, None, None] * core_direction
    new_lith_residual = lith_residual - step_size[:, None] * lith_image
    new_core_residual = core_residual - step_size[:, None, None] * core_image
    norm_after = jnp.sum(new_lith_residual * new_lith_residual, axis=1) + jnp.sum(new_core_residual * new_core_residual, axis=(1, 2))
    conjugacy = norm_after / norm_before
    new_lith_direction = new_lith_residual + conjugacy[:, None] * lith_direction
    new_core_direction = new_core_residual + conjugacy[:, None, None] * core_direction
    return (new_lith_solution, new_lith_residual, new_lith_direction, new_core_solution, new_core_residual, new_core_direction)
```

```python
import jax
import jax.numpy as jnp
from jax import lax
from jax.experimental import pallas as pl
from jax.experimental.pallas import tpu as pltpu
from jax.sharding import PartitionSpec as P

NL, NS, MEM, NJ, JP = 4352, 1024, 64, 55, 56
SEG = 128
WIDE = 1152
MIB = 1 << 20
F32, BF16 = jnp.float32, jnp.bfloat16
VM = pl.BlockSpec(memory_space=pltpu.VMEM)
SM = pl.BlockSpec(memory_space=pltpu.SMEM)
ANY = pl.BlockSpec(memory_space=pl.ANY)
FORWARD_CUTS = (0, 512, 1536, 2560, 3584, 4352)
BACK_CUTS = (0, 512, 1536, 2560, 3584, 4352)
TRANS_B = (((1,), (1,)), ((), ()))


def params(mib):
    return pltpu.CompilerParams(vmem_limit_bytes=mib * MIB)


def struct(shape, dtype=F32):
    return jax.ShapeDtypeStruct(shape, dtype)


def split(values):
    high = values.astype(BF16)
    return high, (values - high.astype(F32)).astype(BF16)


def row_blocks(a_hbm, a_buf, sems, cuts):
    copies = []
    for b in range(len(cuts) - 1):
        rows = pl.ds(cuts[b], cuts[b + 1] - cuts[b])
        copy = pltpu.make_async_copy(a_hbm.at[rows], a_buf.at[rows], sems.at[b])
        copy.start()
        copies.append(copy)
    return copies


def forward_kernel(dir_ref, a_hbm, out_ref, a_buf, lhs, acc, sems):
    copies = row_blocks(a_hbm, a_buf, sems, FORWARD_CUTS)
    high, low = split(dir_ref[...])
    lhs[0:MEM] = high
    lhs[MEM:] = low
    for b, copy in enumerate(copies):
        lo, hi = FORWARD_CUTS[b], FORWARD_CUTS[b + 1]
        copy.wait()
        part = jnp.dot(lhs[:, lo:hi], a_buf[lo:hi], preferred_element_type=F32)
        if b == 0:
            acc[...] = part
        else:
            acc[...] += part
    out_ref[...] = acc[0:MEM] + acc[MEM:]


def spline_values(u):
    now = [jnp.ones_like(u)]
    for d in range(1, 6):
        later = []
        for s in range(d + 1):
            term = 0.0
            if s >= 1:
                term = (u + float(d - s)) * now[s - 1]
            if s < d:
                term = term + (float(s + 1) - u) * now[s]
            later.append(term * (1.0 / d))
        now = later
    return now


def columns_to_rows(cols):
    lane = lax.broadcasted_iota(jnp.int32, (MEM, 128), 1)
    square = jnp.zeros((MEM, 128), F32)
    for k, col in enumerate(cols):
        square = jnp.where(lane == k, col, square)
    square = jnp.concatenate([square, jnp.zeros((128 - MEM, 128), F32)], axis=0)
    return jnp.transpose(square)[0:8]


def core_forward_kernel(
    lith_ref, dir_ref, res_ref, damp_ref, cdir_ref, halo_ref, cres_ref, design_ref, phase_ref,
    knot_ref, cdamp_ref, out_ref, ghi_ref, glo_ref, basis, design, ext,
):
    values = spline_values(phase_ref[...])
    row = lax.broadcasted_iota(jnp.int32, (16, SEG), 0)
    for g in range(8):
        first = lax.rem(knot_ref[g], 8)
        block = jnp.zeros((16, SEG), F32)
        for k in range(6):
            block = block + jnp.where(row == first + k, values[k][g : g + 1, :], 0.0)
        basis[:, g * SEG : (g + 1) * SEG] = block
    design[0:NJ] = design_ref[...].astype(F32)
    design[NJ:JP] = jnp.zeros((1, NS), F32)

    def build(j, carry):
        product = basis[...] * design[pl.ds(j, 1), :]
        high, low = split(product)
        rows = pl.ds(pl.multiple_of(j * 16, 16), 16)
        ghi_ref[rows, :] = high
        glo_ref[rows, :] = low
        return carry

    lax.fori_loop(0, JP, build, 0)
    ext[0:NJ, 0:8, :] = cdir_ref[...]
    ext[0:NJ, 8:16, :] = halo_ref[...]
    ext[NJ:JP] = jnp.zeros((1, 16, MEM), F32)
    high, low = split(jnp.transpose(ext[...].reshape(JP * 16, MEM)))
    both = jnp.concatenate([high, low], axis=0)
    wide = jnp.dot(both, ghi_ref[...], preferred_element_type=F32)
    value = wide[0:MEM] + wide[MEM:] + jnp.dot(high, glo_ref[...], preferred_element_type=F32)
    value = value + lith_ref[...]
    out_ref[...] = jnp.zeros_like(out_ref)
    out_ref[:, :, 0:NS] = value.reshape(8, 8, NS)
    norm = jnp.zeros((8, MEM), F32)
    damped = jnp.zeros((8, MEM), F32)
    for j in range(NJ):
        norm = norm + cres_ref[j] * cres_ref[j]
        damped = damped + cdamp_ref[j] * (cdir_ref[j] * cdir_ref[j])
    lith_norm = jnp.sum(res_ref[...] * res_ref[...], axis=1, keepdims=True)
    lith_damped = jnp.sum(dir_ref[...] * dir_ref[...] * damp_ref[...], axis=1, keepdims=True)
    rows = columns_to_rows([jnp.zeros_like(lith_norm)] * 2 + [lith_norm, lith_damped])
    out_ref[0, :, NS:] = rows
    out_ref[0, 0:1, NS : NS + MEM] = jnp.sum(norm, axis=0, keepdims=True)
    out_ref[0, 1:2, NS : NS + MEM] = jnp.sum(damped, axis=0, keepdims=True)


def core_back_kernel(
    field_ref, weight_ref, ghi_ref, glo_ref, count_ref, pair_ref, local_ref, halo_ref, tile_ref
):
    lane = lax.broadcasted_iota(jnp.int32, (1, SEG), 1)
    curve = jnp.zeros((MEM, SEG), F32)
    for g in range(8):
        cols = slice(g * SEG, (g + 1) * SEG)
        weight = jnp.where(lane < count_ref[g], weight_ref[g : g + 1, :], 0.0)
        field = field_ref[:, :, cols].reshape(MEM, SEG)
        residual = field * weight
        curve = curve + residual * field
        high, low = split(residual)
        pair_ref[0:MEM, cols] = high
        pair_ref[MEM:, cols] = low
    rows = columns_to_rows(
        [jnp.zeros((MEM, 1), F32), jnp.sum(curve, axis=1, keepdims=True)]
    )
    tile_ref[...] = field_ref[0, :, NS:] + rows
    wide = lax.dot_general(ghi_ref[...], pair_ref[...], TRANS_B, preferred_element_type=F32)
    low = lax.dot_general(
        glo_ref[...], pair_ref[0:MEM], TRANS_B, preferred_element_type=F32
    )
    grad = (wide[:, 0:MEM] + wide[:, MEM:] + low).reshape(JP, 16, MEM)
    local_ref[...] = grad[0:NJ, 0:8, :]
    halo_ref[...] = grad[0:NJ, 8:16, :]


def back_kernel(core_ref, pair_ref, a_hbm, own_ref, other_ref, a_buf, lhs, sems):
    copies = row_blocks(a_hbm, a_buf, sems, BACK_CUTS)
    half = MEM // 2
    mine = pl.multiple_of(core_ref[0] * half, half)
    theirs = pl.multiple_of((1 - core_ref[0]) * half, half)
    for k, start in enumerate((mine, theirs, MEM + mine, MEM + theirs)):
        lhs[k * half : (k + 1) * half] = pair_ref[pl.ds(pl.multiple_of(start, half), half), :]
    for out in (own_ref, other_ref):
        out[:, 3, :, NL - 3 * WIDE :] = jnp.zeros((4, 8, 4 * WIDE - NL), F32)
    for b, copy in enumerate(copies):
        lo, hi = BACK_CUTS[b], BACK_CUTS[b + 1]
        copy.wait()
        part = lax.dot_general(lhs[...], a_buf[lo:hi], TRANS_B, preferred_element_type=F32)
        part = part[0:MEM] + part[MEM:]
        edges = sorted({lo, hi} | {e for e in (WIDE, 2 * WIDE, 3 * WIDE) if lo < e < hi})
        for left, right in zip(edges, edges[1:]):
            y = left // WIDE
            place = slice(left - y * WIDE, right - y * WIDE)
            piece = part[:, left - lo : right - lo]
            own_ref[:, y, :, place] = piece[0:half].reshape(4, 8, right - left)
            other_ref[:, y, :, place] = piece[half:].reshape(4, 8, right - left)


def image_kernel(
    own_ref, got_ref, local_ref, halo_ref, cdir_ref, cres_ref, tile_ref, cdamp_ref, out_ref, image_ref
):
    out_ref[...] = own_ref[...] + got_ref[...]
    cross = jnp.zeros((8, MEM), F32)
    square = jnp.zeros((8, MEM), F32)
    for j in range(NJ):
        image = local_ref[j] + halo_ref[j] + cdamp_ref[j] * cdir_ref[j]
        image_ref[j] = image
        cross = cross + cres_ref[j] * image
        square = square + image * image
    out_ref[0, 3, :, NS:] = tile_ref[...]
    out_ref[0, 3, 2:3, NS : NS + MEM] = jnp.sum(cross, axis=0, keepdims=True)
    out_ref[0, 3, 3:4, NS : NS + MEM] = jnp.sum(square, axis=0, keepdims=True)


def turned(row):
    return jnp.transpose(jnp.broadcast_to(row, (128, 128)))


def update_kernel(
    core_ref, own_ref, got_ref, tile_ref, damp_ref, sol_ref, res_ref, dir_ref,
    cimage_ref, csol_ref, cres_ref, cdir_ref,
    new_sol_ref, new_res_ref, new_csol_ref, new_cres_ref, norm_ref, keep_ref, step_col, norm_col,
):
    rt = pl.program_id(0)

    @pl.when(rt == 0)
    def _():
        total = own_ref[0, 3, :, NS:] + got_ref[0, 3, :, NS:]
        before = total[0:1] + tile_ref[2:3]
        curvature = total[1:2] + tile_ref[3:4]
        live = lax.broadcasted_iota(jnp.int32, (1, 128), 1) < MEM
        step = before / jnp.where(live, curvature, 1.0)
        step_col[...] = turned(step)
        keep_ref[0:1] = before
        keep_ref[1:2] = total[0:1]
        keep_ref[2:3] = step * (step * total[3:4] - 2.0 * total[2:3])
        keep_ref[3:8] = jnp.zeros((5, 128), F32)
        step = step[:, 0:MEM]
        for j in range(NJ):
            new_csol_ref[j] = csol_ref[j] + step * cdir_ref[j]
            new_cres_ref[j] = cres_ref[j] - step * cimage_ref[j]

    x = lax.rem(rt, 4)
    step = step_col[pl.ds(pl.multiple_of(rt * 8, 8), 8), 0:1]

    def work(ref):
        image = jnp.concatenate([ref[x, y] for y in range(4)], axis=1)[:, 0:NL]
        direction = dir_ref[...]
        image = image + damp_ref[...] * direction
        new_sol_ref[...] = sol_ref[...] + step * direction
        new_res = res_ref[...] - step * image
        new_res_ref[...] = new_res
        norm = jnp.sum(new_res * new_res, axis=1, keepdims=True)
        norm_col[pl.ds(pl.multiple_of(rt * 8, 8), 8), :] = jnp.broadcast_to(norm, (8, 128))

    mine = rt // 4 == core_ref[0]
    pl.when(mine)(lambda: work(own_ref))
    pl.when(jnp.logical_not(mine))(lambda: work(got_ref))

    @pl.when(rt == 7)
    def _():
        column = jnp.concatenate([norm_col[0:MEM], jnp.zeros((128 - MEM, 128), F32)], axis=0)
        row = jnp.transpose(column)[0:1] + keep_ref[2:3]
        norm_ref[...] = jnp.broadcast_to(row[None], (8, 8, 128))


def direction_kernel(
    norm_ref, keep_ref, res_ref, dir_ref, cres_ref, cdir_ref, new_dir_ref, new_cdir_ref, col
):
    rt = pl.program_id(0)

    @pl.when(rt == 0)
    def _():
        after = norm_ref[0, 0:1]
        for k in range(1, 8):
            after = after + norm_ref[k, 0:1]
        live = lax.broadcasted_iota(jnp.int32, (1, 128), 1) < MEM
        ratio = (after + keep_ref[1:2]) / jnp.where(live, keep_ref[0:1], 1.0)
        col[...] = turned(ratio)
        ratio = ratio[:, 0:MEM]
        for j in range(NJ):
            new_cdir_ref[j] = cres_ref[j] + ratio * cdir_ref[j]

    scale = col[pl.ds(pl.multiple_of(rt * 8, 8), 8), 0:1]
    new_dir_ref[...] = res_ref[...] + scale * dir_ref[...]


def full(shape):
    return pl.BlockSpec(shape, lambda i: (0,) * len(shape))


def shards(
    design_lith, design_core, sample_phase, data_weight, counts, knot_index, lith_damping, core_damping,
    lith_solution, lith_residual, lith_direction, core_solution, core_residual, core_direction,
):
    tm = lax.axis_size("tm")
    core = lax.rem(lax.axis_index("tm"), 2).reshape(1)
    planes = [[t for t in range(tm) if t % 2 == c] for c in range(2)]
    swap = [(t, t ^ 1) for t in range(tm)]
    csol, cres, cdir = (
        jnp.transpose(v, (1, 2, 0)) for v in (core_solution, core_residual, core_direction)
    )
    phase = sample_phase.reshape(8, SEG)
    weight = data_weight.reshape(8, SEG)
    damp = lith_damping.reshape(1, NL)
    upper = lax.ppermute(cdir, "tm", [(t, t - 1) for t in range(1, tm)])

    lith = pl.pallas_call(
        forward_kernel,
        out_shape=struct((MEM, NS)),
        in_specs=[VM, ANY],
        out_specs=VM,
        scratch_shapes=[
            pltpu.VMEM((NL, NS), BF16),
            pltpu.VMEM((2 * MEM, NL), BF16),
            pltpu.VMEM((2 * MEM, NS), F32),
            pltpu.SemaphoreType.DMA((len(FORWARD_CUTS) - 1,)),
        ],
        compiler_params=params(20),
        cost_estimate=pl.CostEstimate(flops=4 * MEM * NL * NS, bytes_accessed=10 * MIB, transcendentals=0),
        name="forward",
    )(lith_direction, design_lith)

    partial, ghi, glo = pl.pallas_call(
        core_forward_kernel,
        out_shape=(struct((8, 8, WIDE)), struct((JP * 16, NS), BF16), struct((JP * 16, NS), BF16)),
        in_specs=[VM] * 9 + [SM] * 2,
        out_specs=(VM, VM, VM),
        scratch_shapes=[
            pltpu.VMEM((16, NS), F32),
            pltpu.VMEM((JP, NS), F32),
            pltpu.VMEM((JP, 16, MEM), F32),
        ],
        compiler_params=params(16),
        name="core_forward",
    )(
        lith, lith_direction, lith_residual, damp, cdir, upper, cres, design_core, phase,
        knot_index, core_damping,
    )

    parts = lax.all_to_all(partial, "coef", 0, 0)
    field = lax.all_to_all(
        jnp.broadcast_to(jnp.sum(parts, axis=0)[None], (8, 8, WIDE)), "coef", 0, 0
    )

    pair, local, halo, tile = pl.pallas_call(
        core_back_kernel,
        out_shape=(
            struct((2 * MEM, NS), BF16),
            struct((NJ, 8, MEM)),
            struct((NJ, 8, MEM)),
            struct((8, 128)),
        ),
        in_specs=[VM] * 4 + [SM],
        out_specs=(VM,) * 4,
        compiler_params=params(16),
        name="core_back",
    )(field, weight, ghi, glo, counts)
    lower = lax.ppermute(halo, "tm", [(t, t + 1) for t in range(tm - 1)])

    own, other = pl.pallas_call(
        back_kernel,
        out_shape=(struct((4, 4, 8, WIDE)), struct((4, 4, 8, WIDE))),
        in_specs=[SM, VM, ANY],
        out_specs=(VM, VM),
        scratch_shapes=[
            pltpu.VMEM((NL, NS), BF16),
            pltpu.VMEM((2 * MEM, NS), BF16),
            pltpu.SemaphoreType.DMA((len(BACK_CUTS) - 1,)),
        ],
        compiler_params=params(20),
        cost_estimate=pl.CostEstimate(flops=4 * MEM * NL * NS, bytes_accessed=10 * MIB, transcendentals=0),
        name="back",
    )(core, pair, design_lith)
    got = lax.ppermute(other, "tm", swap)

    terms, cimage = pl.pallas_call(
        image_kernel,
        out_shape=(struct((4, 4, 8, WIDE)), struct((NJ, 8, MEM))),
        in_specs=[VM] * 7 + [SM],
        out_specs=(VM, VM),
        compiler_params=params(12),
        name="image",
    )(own, got, local, lower, cdir, cres, tile, core_damping)

    pieces = lax.all_to_all(
        terms.reshape(16, 8, WIDE), "tm", 0, 0, axis_index_groups=planes
    )
    whole = lax.all_to_all(
        jnp.broadcast_to(jnp.sum(pieces, axis=0)[None], (16, 8, WIDE)),
        "tm", 0, 0, axis_index_groups=planes,
    ).reshape(4, 4, 8, WIDE)
    rest = lax.ppermute(whole, "tm", swap)

    lith_block = pl.BlockSpec((8, NL), lambda i: (i, 0))
    core_full = full((NJ, 8, MEM))
    chunk_full = full((4, 4, 8, WIDE))
    lith_struct = struct((MEM, NL))
    core_struct = struct((NJ, 8, MEM))
    z_tile = field[0, :, NS:]
    new_sol, new_res, new_csol, new_cres, norms, keep = pl.pallas_call(
        update_kernel,
        grid=(8,),
        out_shape=(
            lith_struct, lith_struct, core_struct, core_struct, struct((8, 8, 128)), struct((8, 128))
        ),
        in_specs=[SM, chunk_full, chunk_full, full((8, 128)), full((1, NL))]
        + [lith_block] * 3
        + [core_full] * 4,
        out_specs=(lith_block, lith_block, core_full, core_full, full((8, 8, 128)), full((8, 128))),
        scratch_shapes=[pltpu.VMEM((128, 128), F32), pltpu.VMEM((128, 128), F32)],
        compiler_params=params(16),
        name="update",
    )(
        core, whole, rest, z_tile, damp, lith_solution, lith_residual, lith_direction,
        cimage, csol, cres, cdir,
    )
    norms = lax.all_to_all(norms, "coef", 0, 0)
    new_dir, new_cdir = pl.pallas_call(
        direction_kernel,
        grid=(8,),
        out_shape=(lith_struct, core_struct),
        in_specs=[full((8, 8, 128)), full((8, 128)), lith_block, lith_block, core_full, core_full],
        out_specs=(lith_block, core_full),
        scratch_shapes=[pltpu.VMEM((128, 128), F32)],
        compiler_params=params(12),
        name="direction",
    )(norms, keep, new_res, lith_direction, new_cres, cdir)
    back = lambda v: jnp.transpose(v, (2, 0, 1))
    return new_sol, new_res, new_dir, back(new_csol), back(new_cres), back(new_cdir)


def solution(mesh):
    lith, core = P(None, "coef"), P(None, "coef", "tm")
    return jax.shard_map(
        shards,
        mesh=mesh,
        in_specs=(
            P("coef", "tm"), P("coef", "tm"), P("tm"), P("tm"), P("tm"), P("tm"), P("coef"), P("coef"),
            lith, lith, lith, core, core, core,
        ),
        out_specs=(lith, lith, lith, core, core, core),
        check_vma=False,
    )
```

```python
import jax
import jax.numpy as jnp
from jax import lax
from jax.experimental import pallas as pl
from jax.experimental.pallas import tpu as pltpu
from jax.sharding import PartitionSpec as P

NL, NS, MEM, NJ, JP = 4352, 1024, 64, 55, 56
SEG = 128
WIDE, SENT = 1152, 1280
MIB = 1 << 20
F32, BF16 = jnp.float32, jnp.bfloat16
VM = pl.BlockSpec(memory_space=pltpu.VMEM)
SM = pl.BlockSpec(memory_space=pltpu.SMEM)
HB = pl.BlockSpec(memory_space=pltpu.HBM)
FORWARD_CUTS = (0, 512, 1280, 2304, 3328, 4352)
TRANS_B = (((1,), (1,)), ((), ()))


def params(mib):
    return pltpu.CompilerParams(vmem_limit_bytes=mib * MIB)


def struct(shape, dtype=F32):
    return jax.ShapeDtypeStruct(shape, dtype)


def split(values):
    high = values.astype(BF16)
    return high, (values - high.astype(F32)).astype(BF16)


def spline_values(u):
    now = [jnp.ones_like(u)]
    for d in range(1, 6):
        later = []
        for s in range(d + 1):
            term = 0.0
            if s >= 1:
                term = (u + float(d - s)) * now[s - 1]
            if s < d:
                term = term + (float(s + 1) - u) * now[s]
            later.append(term * (1.0 / d))
        now = later
    return now


def forward_kernel(
    dir_hbm, a_hbm, design_hbm, phase_hbm, knot_hbm, out_ref, a_buf, ghi_ref, glo_ref,
    dir_buf, lhs, acc, design_buf, phase_buf, knot_buf, basis, design, small_sems, sems,
):
    small = [
        pltpu.make_async_copy(src, dst, small_sems.at[k])
        for k, (src, dst) in enumerate(
            ((phase_hbm, phase_buf), (knot_hbm, knot_buf), (design_hbm, design_buf), (dir_hbm, dir_buf))
        )
    ]
    for copy in small:
        copy.start()
    copies = []
    for b in range(len(FORWARD_CUTS) - 1):
        rows = pl.ds(FORWARD_CUTS[b], FORWARD_CUTS[b + 1] - FORWARD_CUTS[b])
        copy = pltpu.make_async_copy(a_hbm.at[rows], a_buf.at[rows], sems.at[b])
        copy.start()
        copies.append(copy)
    for copy in small[0:3]:
        copy.wait()
    values = spline_values(phase_buf[...])
    row = lax.broadcasted_iota(jnp.int32, (16, SEG), 0)
    for g in range(8):
        first = lax.rem(knot_buf[g], 8)
        block = jnp.zeros((16, SEG), F32)
        for k in range(6):
            block = block + jnp.where(row == first + k, values[k][g : g + 1, :], 0.0)
        basis[:, g * SEG : (g + 1) * SEG] = block
    design[0:NJ] = design_buf[...].astype(F32)
    design[NJ:JP] = jnp.zeros((1, NS), F32)

    def build(j, carry):
        high, low = split(basis[...] * design[pl.ds(j, 1), :])
        rows = pl.ds(pl.multiple_of(j * 16, 16), 16)
        ghi_ref[rows, :] = high
        glo_ref[rows, :] = low
        return carry

    lax.fori_loop(0, JP, build, 0)
    small[3].wait()
    for b, copy in enumerate(copies):
        lo, hi = FORWARD_CUTS[b], FORWARD_CUTS[b + 1]
        high, low = split(dir_buf[:, lo:hi])
        lhs[0:MEM, lo:hi] = high
        lhs[MEM:, lo:hi] = low
        copy.wait()
        part = jnp.dot(lhs[:, lo:hi], a_buf[lo:hi], preferred_element_type=F32)
        if b == 0:
            acc[...] = part
        else:
            acc[...] += part
    out_ref[...] = acc[0:MEM] + acc[MEM:]


def core_forward_kernel(lith_ref, cdir_ref, halo_ref, ghi_ref, glo_ref, out_ref, ext):
    ext[0:NJ, 0:8, :] = cdir_ref[...]
    ext[0:NJ, 8:16, :] = halo_ref[...]
    ext[NJ:JP] = jnp.zeros((1, 16, MEM), F32)
    high, low = split(jnp.transpose(ext[...].reshape(JP * 16, MEM)))
    both = jnp.concatenate([high, low], axis=0)
    wide = jnp.dot(both, ghi_ref[...], preferred_element_type=F32)
    value = wide[0:MEM] + wide[MEM:] + jnp.dot(high, glo_ref[...], preferred_element_type=F32)
    out_ref[...] = (value + lith_ref[...]).reshape(8, 8, NS)


def sum_kernel(parts_ref, out_ref):
    total = parts_ref[0]
    for k in range(1, parts_ref.shape[0]):
        total = total + parts_ref[k]
    for k in range(parts_ref.shape[0]):
        out_ref[k] = total


def core_back_kernel(
    field_ref, weight_ref, ghi_ref, glo_ref, count_ref, pair_ref, local_ref, halo_ref, curve_ref
):
    lane = lax.broadcasted_iota(jnp.int32, (1, SEG), 1)
    curve = jnp.zeros((MEM, SEG), F32)
    for g in range(8):
        cols = slice(g * SEG, (g + 1) * SEG)
        weight = jnp.where(lane < count_ref[g], weight_ref[g : g + 1, :], 0.0)
        field = field_ref[:, :, cols].reshape(MEM, SEG)
        residual = field * weight
        curve = curve + residual * field
        high, low = split(residual)
        pair_ref[0:MEM, cols] = high
        pair_ref[MEM:, cols] = low
    curve_ref[...] = curve
    wide = lax.dot_general(ghi_ref[...], pair_ref[...], TRANS_B, preferred_element_type=F32)
    low = lax.dot_general(
        glo_ref[...], pair_ref[0:MEM], TRANS_B, preferred_element_type=F32
    )
    grad = (wide[:, 0:MEM] + wide[:, MEM:] + low).reshape(JP, 16, MEM)
    local_ref[...] = grad[0:NJ, 0:8, :]
    halo_ref[...] = grad[0:NJ, 8:16, :]


def back_kernel(pair_ref, a_ref, own_ref, other_ref, lhs):
    half = MEM // 2
    core = lax.axis_index("core")
    mine = pl.multiple_of(core * half, half)
    theirs = pl.multiple_of((1 - core) * half, half)
    for k, start in enumerate((mine, theirs, MEM + mine, MEM + theirs)):
        lhs[k * half : (k + 1) * half] = pair_ref[pl.ds(pl.multiple_of(start, half), half), :]
    for y in range(4):
        cols = columns_of(y)
        count = cols.stop - cols.start
        part = lax.dot_general(lhs[...], a_ref[cols], TRANS_B, preferred_element_type=F32)
        part = part[0:MEM] + part[MEM:]
        own_ref[:, y, :, 0:count] = part[0:half].reshape(4, 8, count)
        other_ref[:, y, :, 0:count] = part[half:].reshape(4, 8, count)
    for out in (own_ref, other_ref):
        out[:, 3, :, NL - 3 * WIDE :] = jnp.zeros((4, 8, 4 * WIDE - NL), F32)


def add_kernel(a_ref, b_ref, out_ref):
    out_ref[...] = a_ref[...] + b_ref[...]


def turned(row):
    return jnp.transpose(jnp.broadcast_to(row, (128, 128)))


def columns_of(y):
    return slice(y * WIDE, min((y + 1) * WIDE, NL))


def out_copies(pairs, sems):
    copies = [
        pltpu.make_async_copy(src, dst, sems.at[k]) for k, (src, dst) in enumerate(pairs)
    ]
    for copy in copies:
        copy.start()
    return copies


def damp_rows(damp_ref, cols):
    rows = range(cols.start // SEG, cols.stop // SEG)
    return jnp.concatenate(
        [jnp.broadcast_to(damp_ref[t : t + 1, :], (8, SEG)) for t in rows], axis=1
    )


def folded(values):
    total = values[:, 0:SEG]
    for t in range(1, values.shape[1] // SEG):
        total = total + values[:, t * SEG : (t + 1) * SEG]
    return total


def member_row(columns):
    padded = jnp.concatenate([columns, jnp.zeros((128 - MEM, 128), F32)], axis=0)
    return jnp.sum(jnp.transpose(padded), axis=0, keepdims=True)[:, 0:MEM]


def image_kernel(
    parts_ref, local_ref, halo_ref, cdir_ref, cres_ref, curve_ref, dir_ref, res_ref, damp_ref, cdamp_ref,
    chunk_ref, cimage_ref, sums_ref, square,
):
    zero = jnp.zeros((8, MEM), F32)
    before, curve, cross, norm = zero, zero, zero, zero
    for j in range(NJ):
        residual = cres_ref[j]
        damped = cdamp_ref[j] * cdir_ref[j]
        core_image = local_ref[j] + halo_ref[j] + damped
        cimage_ref[j] = core_image
        before = before + residual * residual
        curve = curve + damped * cdir_ref[j]
        cross = cross + residual * core_image
        norm = norm + core_image * core_image
    total = parts_ref[0]
    for k in range(1, 16):
        total = total + parts_ref[k]
    chunk_ref[...] = total
    square[...] = jnp.zeros((2, MEM, 128), F32)
    plane = lax.axis_index("plane")
    core = lax.axis_index("core")
    rows = pl.ds(pl.multiple_of((core * 4 + plane // 4) * 8, 8), 8)

    def finish(y):
        cols = columns_of(y)
        count = cols.stop - cols.start
        value = chunk_ref[:, 0:count] + damp_rows(damp_ref, cols) * dir_ref[rows, cols]
        chunk_ref[:, 0:count] = value
        square[0, rows, :] = folded(value * res_ref[rows, cols])
        square[1, rows, :] = folded(value * value)

    for y in range(4):
        pl.when(lax.rem(plane, 4) == y)(lambda y=y: finish(y))
    lith_before = jnp.zeros((MEM, SEG), F32)
    lith_curve = jnp.zeros((MEM, SEG), F32)
    for t in range(NL // SEG):
        cols = slice(t * SEG, (t + 1) * SEG)
        lith_before = lith_before + res_ref[:, cols] * res_ref[:, cols]
        lith_curve = lith_curve + dir_ref[:, cols] * dir_ref[:, cols] * damp_ref[t : t + 1, :]
    once = jnp.where(jnp.logical_and(plane == 0, core == 0), 1.0, 0.0)
    first = jnp.where(lax.axis_index("coef") == 0, 1.0, 0.0)
    lith_curve = once * lith_curve + first * curve_ref[...]
    rows_of = [
        (before, once * lith_before), (curve, lith_curve), (cross, square[0]), (norm, square[1])
    ]
    tile = jnp.concatenate(
        [jnp.sum(c, axis=0, keepdims=True) + member_row(v) for c, v in rows_of]
        + [jnp.zeros((4, MEM), F32)],
        axis=0,
    )
    tile = jnp.concatenate([tile, jnp.zeros((8, 128 - MEM), F32)], axis=1)
    for k in range(8):
        sums_ref[k] = tile


def spread_kernel(sums_ref, chunk_ref, out_ref):
    tile = sums_ref[0]
    for k in range(1, 8):
        tile = tile + sums_ref[k]
    for k in range(16):
        out_ref[k, :, 0:WIDE] = chunk_ref[...]
        out_ref[k, :, WIDE:] = tile


def update_kernel(
    own_ref, got_ref, sol_ref, res_ref, dir_ref, cimage_ref, csol_ref, cres_ref, cdir_ref,
    sol_hbm, res_hbm, dir_hbm, csol_hbm, cres_hbm, cdir_hbm,
    sol_buf, res_buf, dir_buf, csol_buf, cres_buf, cdir_buf, step_col, ratio_col, core_sems, sems,
):
    core = lax.axis_index("core")
    tile = jnp.zeros((8, 128), F32)
    for x in range(4):
        for y in range(4):
            tile = tile + (own_ref[x, y, :, WIDE:] + got_ref[x, y, :, WIDE:])
    tile = tile[:, 0:MEM]
    before = tile[0:1]
    step = before / tile[1:2]
    ratio = (before + step * (step * tile[3:4] - 2.0 * tile[2:3])) / before
    blank = jnp.zeros((1, 128 - MEM), F32)
    step_col[...] = turned(jnp.concatenate([step, blank], axis=1))
    ratio_col[...] = turned(jnp.concatenate([ratio, blank], axis=1))
    waits = []
    for y in range(4):
        cols = columns_of(y)
        count = (cols.stop - cols.start) // SEG
        for k in range(8):
            ref, part = (own_ref, core) if k < 4 else (got_ref, 1 - core)
            rows = pl.ds(pl.multiple_of(part * 32 + (k % 4) * 8, 8), 8)
            scale = jnp.concatenate([step_col[rows, :]] * count, axis=1)
            other = jnp.concatenate([ratio_col[rows, :]] * count, axis=1)
            direction = dir_ref[rows, cols]
            sol_buf[rows, cols] = sol_ref[rows, cols] + scale * direction
            new_res = res_ref[rows, cols] - scale * ref[k % 4, y, :, 0 : count * SEG]
            res_buf[rows, cols] = new_res
            dir_buf[rows, cols] = new_res + other * direction
        waits += out_copies(
            [
                (buf.at[:, cols], hbm.at[:, cols])
                for buf, hbm in ((sol_buf, sol_hbm), (res_buf, res_hbm), (dir_buf, dir_hbm))
            ],
            sems.at[y],
        )
    for j in range(NJ):
        csol_buf[j] = csol_ref[j] + step * cdir_ref[j]
        new_res = cres_ref[j] - step * cimage_ref[j]
        cres_buf[j] = new_res
        cdir_buf[j] = new_res + ratio * cdir_ref[j]
    waits += out_copies(
        [(csol_buf, csol_hbm), (cres_buf, cres_hbm), (cdir_buf, cdir_hbm)], core_sems
    )
    for copy in waits:
        copy.wait()


def shards(
    design_lith, design_core, sample_phase, data_weight, counts, knot_index, lith_damping, core_damping,
    lith_solution, lith_residual, lith_direction, core_solution, core_residual, core_direction,
):
    segments = ("plane", "core")
    tm = lax.axis_size("plane") * 2
    swap = [(0, 1), (1, 0)]
    csol, cres, cdir = (
        jnp.transpose(v, (1, 2, 0)) for v in (core_solution, core_residual, core_direction)
    )
    phase = sample_phase.reshape(8, SEG)
    weight = data_weight.reshape(8, SEG)
    damp = lith_damping.reshape(NL // SEG, SEG)
    upper = lax.ppermute(cdir, segments, [(t, t - 1) for t in range(1, tm)])
    product_cost = pl.CostEstimate(
        flops=16 * MEM * NL * NS, bytes_accessed=12 * MIB, transcendentals=0
    )

    pin = lambda v: pltpu.with_memory_space_constraint(v, pltpu.HBM)
    lith, design, ghi, glo = pl.pallas_call(
        forward_kernel,
        out_shape=(
            struct((MEM, NS)),
            pltpu.VMEM((NL, NS), BF16),
            struct((JP * 16, NS), BF16),
            struct((JP * 16, NS), BF16),
        ),
        in_specs=[HB] * 5,
        out_specs=(VM,) * 4,
        scratch_shapes=[
            pltpu.VMEM((MEM, NL), F32),
            pltpu.VMEM((2 * MEM, NL), BF16),
            pltpu.VMEM((2 * MEM, NS), F32),
            pltpu.VMEM((NJ, NS), BF16),
            pltpu.VMEM((8, SEG), F32),
            pltpu.SMEM((8,), jnp.int32),
            pltpu.VMEM((16, NS), F32),
            pltpu.VMEM((JP, NS), F32),
            pltpu.SemaphoreType.DMA((4,)),
            pltpu.SemaphoreType.DMA((len(FORWARD_CUTS) - 1,)),
        ],
        compiler_params=params(24),
        cost_estimate=product_cost,
        name="forward",
    )(pin(lith_direction), pin(design_lith), pin(design_core), pin(phase), pin(knot_index))

    partial = pl.pallas_call(
        core_forward_kernel,
        out_shape=struct((8, 8, NS)),
        in_specs=[VM] * 5,
        out_specs=VM,
        scratch_shapes=[pltpu.VMEM((JP, 16, MEM), F32)],
        compiler_params=params(12),
        name="core_forward",
    )(lith, cdir, upper, ghi, glo)

    parts = lax.all_to_all(partial, "coef", 0, 0)
    total = pl.pallas_call(
        sum_kernel,
        out_shape=struct(parts.shape),
        in_specs=[VM],
        out_specs=VM,
        compiler_params=params(8),
        name="field_sum",
    )(parts)
    field = lax.all_to_all(total, "coef", 0, 0)

    pair, local, halo, curve = pl.pallas_call(
        core_back_kernel,
        out_shape=(
            struct((2 * MEM, NS), BF16),
            struct((NJ, 8, MEM)),
            struct((NJ, 8, MEM)),
            struct((MEM, SEG)),
        ),
        in_specs=[VM] * 4 + [SM],
        out_specs=(VM,) * 4,
        compiler_params=params(16),
        name="core_back",
    )(field, weight, ghi, glo, counts)
    lower = lax.ppermute(halo, segments, [(t, t + 1) for t in range(tm - 1)])

    chunks = struct((4, 4, 8, WIDE))
    core_struct = struct((NJ, 8, MEM))
    own, other = pl.pallas_call(
        back_kernel,
        out_shape=(chunks, chunks),
        in_specs=[VM, VM],
        out_specs=(VM, VM),
        scratch_shapes=[pltpu.VMEM((2 * MEM, NS), BF16)],
        compiler_params=params(12),
        cost_estimate=product_cost,
        name="back",
    )(pair, design)
    other, lower = lax.optimization_barrier((other, lower))
    got = lax.ppermute(other, "core", swap)
    terms = pl.pallas_call(
        add_kernel,
        out_shape=chunks,
        in_specs=[VM, VM],
        out_specs=VM,
        compiler_params=params(8),
        name="add_halves",
    )(own, got)

    pieces = lax.all_to_all(terms.reshape(16, 8, WIDE), "plane", 0, 0)
    chunk, cimage, sums = pl.pallas_call(
        image_kernel,
        out_shape=(struct((8, WIDE)), core_struct, struct((8, 8, 128))),
        in_specs=[VM] * 9 + [SM],
        out_specs=(VM, VM, VM),
        scratch_shapes=[pltpu.VMEM((2, MEM, 128), F32)],
        compiler_params=params(12),
        name="image",
    )(pieces, local, lower, cdir, cres, curve, lith_direction, lith_residual, damp, core_damping)
    sums = lax.all_to_all(sums, "coef", 0, 0)
    sent = pl.pallas_call(
        spread_kernel,
        out_shape=struct((16, 8, SENT)),
        in_specs=[VM, VM],
        out_specs=VM,
        compiler_params=params(8),
        name="spread",
    )(sums, chunk)
    whole = lax.all_to_all(sent, "plane", 0, 0).reshape(4, 4, 8, SENT)
    rest = lax.ppermute(whole, "core", swap)

    lith_struct = struct((MEM, NL))
    new_sol, new_res, new_dir, new_csol, new_cres, new_cdir = pl.pallas_call(
        update_kernel,
        out_shape=(lith_struct,) * 3 + (core_struct,) * 3,
        in_specs=[VM] * 9,
        out_specs=(HB,) * 6,
        scratch_shapes=[pltpu.VMEM((MEM, NL), F32)] * 3
        + [pltpu.VMEM((NJ, 8, MEM), F32)] * 3
        + [pltpu.VMEM((128, 128), F32)] * 2
        + [pltpu.SemaphoreType.DMA((3,)), pltpu.SemaphoreType.DMA((4, 3))],
        compiler_params=params(20),
        name="update",
    )(
        whole, rest, lith_solution, lith_residual, lith_direction, cimage, csol, cres, cdir,
    )
    back = lambda v: jnp.transpose(v, (2, 0, 1))
    return new_sol, new_res, new_dir, back(new_csol), back(new_cres), back(new_cdir)


def solution(mesh):
    parts = jax.sharding.Mesh(mesh.devices.reshape(-1, 2, mesh.devices.shape[1]), ("plane", "core", "coef"))
    segments = ("plane", "core")
    lith, core = P(None, "coef"), P(None, "coef", segments)
    return jax.shard_map(
        shards,
        mesh=parts,
        in_specs=(
            P("coef", segments), P("coef", segments), P(segments), P(segments), P(segments), P(segments),
            P("coef"), P("coef"), lith, lith, lith, core, core, core,
        ),
        out_specs=(lith, lith, lith, core, core, core),
        check_vma=False,
    )
```

```python
import jax
import jax.numpy as jnp
from jax import lax
from jax.experimental import pallas as pl
from jax.experimental.pallas import tpu as pltpu
from jax.sharding import PartitionSpec as P

NL, NS, MEM, NJ, JP = 4352, 1024, 64, 55, 56
SEG = 128
WIDE, SENT = 1152, 1280
MIB = 1 << 20
F32, BF16 = jnp.float32, jnp.bfloat16
VM = pl.BlockSpec(memory_space=pltpu.VMEM)
SM = pl.BlockSpec(memory_space=pltpu.SMEM)
HB = pl.BlockSpec(memory_space=pltpu.HBM)
FORWARD_CUTS = (0, 512, 1280, 2304, 3328, 4352)
TRANS_B = (((1,), (1,)), ((), ()))


def params(mib):
    return pltpu.CompilerParams(vmem_limit_bytes=mib * MIB)


def struct(shape, dtype=F32):
    return jax.ShapeDtypeStruct(shape, dtype)


def split(values):
    high = values.astype(BF16)
    return high, (values - high.astype(F32)).astype(BF16)


def spline_values(u):
    now = [jnp.ones_like(u)]
    for d in range(1, 6):
        later = []
        for s in range(d + 1):
            term = 0.0
            if s >= 1:
                term = (u + float(d - s)) * now[s - 1]
            if s < d:
                term = term + (float(s + 1) - u) * now[s]
            later.append(term * (1.0 / d))
        now = later
    return now


def forward_kernel(
    dir_hbm, a_hbm, design_hbm, phase_hbm, knot_hbm, out_ref, a_buf, ghi_ref, glo_ref,
    dir_buf, lhs, acc, design_buf, phase_buf, knot_buf, basis, design, small_sems, sems,
):
    small = [
        pltpu.make_async_copy(src, dst, small_sems.at[k])
        for k, (src, dst) in enumerate(
            ((phase_hbm, phase_buf), (knot_hbm, knot_buf), (design_hbm, design_buf), (dir_hbm, dir_buf))
        )
    ]
    for copy in small:
        copy.start()
    copies = []
    for b in range(len(FORWARD_CUTS) - 1):
        rows = pl.ds(FORWARD_CUTS[b], FORWARD_CUTS[b + 1] - FORWARD_CUTS[b])
        copy = pltpu.make_async_copy(a_hbm.at[rows], a_buf.at[rows], sems.at[b])
        copy.start()
        copies.append(copy)
    for copy in small[0:3]:
        copy.wait()
    values = spline_values(phase_buf[...])
    row = lax.broadcasted_iota(jnp.int32, (16, SEG), 0)
    for g in range(8):
        first = lax.rem(knot_buf[g], 8)
        block = jnp.zeros((16, SEG), F32)
        for k in range(6):
            block = block + jnp.where(row == first + k, values[k][g : g + 1, :], 0.0)
        basis[:, g * SEG : (g + 1) * SEG] = block
    design[0:NJ] = design_buf[...].astype(F32)
    design[NJ:JP] = jnp.zeros((1, NS), F32)

    def build(j, carry):
        high, low = split(basis[...] * design[pl.ds(j, 1), :])
        rows = pl.ds(pl.multiple_of(j * 16, 16), 16)
        ghi_ref[rows, :] = high
        glo_ref[rows, :] = low
        return carry

    lax.fori_loop(0, JP, build, 0)
    small[3].wait()
    for b, copy in enumerate(copies):
        lo, hi = FORWARD_CUTS[b], FORWARD_CUTS[b + 1]
        high, low = split(dir_buf[:, lo:hi])
        lhs[0:MEM, lo:hi] = high
        lhs[MEM:, lo:hi] = low
        copy.wait()
        part = jnp.dot(lhs[:, lo:hi], a_buf[lo:hi], preferred_element_type=F32)
        if b == 0:
            acc[...] = part
        else:
            acc[...] += part
    out_ref[...] = acc[0:MEM] + acc[MEM:]


def core_forward_kernel(lith_ref, cdir_ref, halo_ref, ghi_ref, glo_ref, out_ref, ext):
    ext[0:NJ, 0:8, :] = cdir_ref[...]
    last = jnp.logical_and(lax.axis_index("plane") == 15, lax.axis_index("core") == 1)
    ext[0:NJ, 8:16, :] = halo_ref[...] * jnp.where(last, 0.0, 1.0)
    ext[NJ:JP] = jnp.zeros((1, 16, MEM), F32)
    high, low = split(jnp.transpose(ext[...].reshape(JP * 16, MEM)))
    both = jnp.concatenate([high, low], axis=0)
    wide = jnp.dot(both, ghi_ref[...], preferred_element_type=F32)
    value = wide[0:MEM] + wide[MEM:] + jnp.dot(high, glo_ref[...], preferred_element_type=F32)
    out_ref[...] = (value + lith_ref[...]).reshape(8, 8, NS)


def sum_kernel(parts_ref, out_ref):
    total = parts_ref[0]
    for k in range(1, parts_ref.shape[0]):
        total = total + parts_ref[k]
    for k in range(parts_ref.shape[0]):
        out_ref[k] = total


def core_back_kernel(
    field_ref, weight_ref, ghi_ref, glo_ref, count_ref, pair_ref, local_ref, halo_ref, curve_ref
):
    lane = lax.broadcasted_iota(jnp.int32, (1, SEG), 1)
    curve = jnp.zeros((MEM, SEG), F32)
    for g in range(8):
        cols = slice(g * SEG, (g + 1) * SEG)
        weight = jnp.where(lane < count_ref[g], weight_ref[g : g + 1, :], 0.0)
        field = field_ref[:, :, cols].reshape(MEM, SEG)
        residual = field * weight
        curve = curve + residual * field
        high, low = split(residual)
        pair_ref[0:MEM, cols] = high
        pair_ref[MEM:, cols] = low
    curve_ref[...] = curve
    wide = lax.dot_general(ghi_ref[...], pair_ref[...], TRANS_B, preferred_element_type=F32)
    low = lax.dot_general(
        glo_ref[...], pair_ref[0:MEM], TRANS_B, preferred_element_type=F32
    )
    grad = (wide[:, 0:MEM] + wide[:, MEM:] + low).reshape(JP, 16, MEM)
    local_ref[...] = grad[0:NJ, 0:8, :]
    halo_ref[...] = jnp.concatenate([grad[0 : JP // 2, 8:16, :], grad[JP // 2 :, 8:16, :]], axis=2)


def back_kernel(pair_ref, a_ref, own_ref, other_ref, lhs):
    half = MEM // 2
    core = lax.axis_index("core")
    mine = pl.multiple_of(core * half, half)
    theirs = pl.multiple_of((1 - core) * half, half)
    for k, start in enumerate((mine, theirs, MEM + mine, MEM + theirs)):
        lhs[k * half : (k + 1) * half] = pair_ref[pl.ds(pl.multiple_of(start, half), half), :]
    for y in range(4):
        cols = columns_of(y)
        count = cols.stop - cols.start
        part = lax.dot_general(lhs[...], a_ref[cols], TRANS_B, preferred_element_type=F32)
        part = part[0:MEM] + part[MEM:]
        own_ref[:, y, :, 0:count] = part[0:half].reshape(4, 8, count)
        other_ref[:, y, :, 0:count] = part[half:].reshape(4, 8, count)
    for out in (own_ref, other_ref):
        out[:, 3, :, NL - 3 * WIDE :] = jnp.zeros((4, 8, 4 * WIDE - NL), F32)


def add_kernel(
    a_ref, b_ref, tile_ref, local_ref, halo_ref, cdir_ref, cres_ref, cdamp_ref, out_ref, tile_out_ref, cimage_ref
):
    out_ref[...] = a_ref[...] + b_ref[...]
    cross = jnp.zeros((8, MEM), F32)
    norm = jnp.zeros((8, MEM), F32)
    first = jnp.logical_and(lax.axis_index("plane") == 0, lax.axis_index("core") == 0)
    later = jnp.where(first, 0.0, 1.0)
    for j in range(NJ):
        packed = halo_ref[j % (JP // 2)]
        halo = packed[:, 0:MEM] if j < JP // 2 else packed[:, MEM:]
        core_image = local_ref[j] + later * halo + cdamp_ref[j] * cdir_ref[j]
        cimage_ref[j] = core_image
        cross = cross + cres_ref[j] * core_image
        norm = norm + core_image * core_image
    zero = jnp.zeros((1, MEM), F32)
    tile_out_ref[...] = tile_ref[...] + tile_of(
        [zero, zero, jnp.sum(cross, axis=0, keepdims=True), jnp.sum(norm, axis=0, keepdims=True)]
    )


def turned(row):
    return jnp.transpose(jnp.broadcast_to(row, (128, 128)))


def columns_of(y):
    return slice(y * WIDE, min((y + 1) * WIDE, NL))


def out_copies(pairs, sems):
    copies = [
        pltpu.make_async_copy(src, dst, sems.at[k]) for k, (src, dst) in enumerate(pairs)
    ]
    for copy in copies:
        copy.start()
    return copies


def damp_rows(damp_ref, cols):
    rows = range(cols.start // SEG, cols.stop // SEG)
    return jnp.concatenate(
        [jnp.broadcast_to(damp_ref[t : t + 1, :], (8, SEG)) for t in rows], axis=1
    )


def folded(values):
    total = values[:, 0:SEG]
    for t in range(1, values.shape[1] // SEG):
        total = total + values[:, t * SEG : (t + 1) * SEG]
    return total


def member_row(columns):
    padded = jnp.concatenate([columns, jnp.zeros((128 - MEM, 128), F32)], axis=0)
    return jnp.sum(jnp.transpose(padded), axis=0, keepdims=True)[:, 0:MEM]


def tile_of(rows):
    tile = jnp.concatenate(rows + [jnp.zeros((8 - len(rows), MEM), F32)], axis=0)
    return jnp.concatenate([tile, jnp.zeros((8, 128 - MEM), F32)], axis=1)


def known_sums_kernel(cdir_ref, cres_ref, dir_ref, res_ref, damp_ref, cdamp_ref, tile_ref):
    before = jnp.zeros((8, MEM), F32)
    curve = jnp.zeros((8, MEM), F32)
    for j in range(NJ):
        before = before + cres_ref[j] * cres_ref[j]
        curve = curve + cdamp_ref[j] * (cdir_ref[j] * cdir_ref[j])
    lith_before = jnp.zeros((MEM, SEG), F32)
    lith_curve = jnp.zeros((MEM, SEG), F32)
    for t in range(NL // SEG):
        cols = slice(t * SEG, (t + 1) * SEG)
        lith_before = lith_before + res_ref[:, cols] * res_ref[:, cols]
        lith_curve = lith_curve + dir_ref[:, cols] * dir_ref[:, cols] * damp_ref[t : t + 1, :]
    once = jnp.logical_and(lax.axis_index("plane") == 0, lax.axis_index("core") == 0)
    once = jnp.where(once, 1.0, 0.0)
    tile_ref[...] = tile_of(
        [
            jnp.sum(c, axis=0, keepdims=True) + once * member_row(v)
            for c, v in ((before, lith_before), (curve, lith_curve))
        ]
    )


def image_kernel(parts_ref, curve_ref, dir_ref, res_ref, damp_ref, tile_ref, out_ref, image, square):
    total = parts_ref[0]
    for k in range(1, 16):
        total = total + parts_ref[k]
    image[...] = total
    square[...] = jnp.zeros((2, MEM, 128), F32)
    plane = lax.axis_index("plane")
    rows = pl.ds(pl.multiple_of((lax.axis_index("core") * 4 + plane // 4) * 8, 8), 8)

    def finish(y):
        cols = columns_of(y)
        count = cols.stop - cols.start
        value = image[:, 0:count] + damp_rows(damp_ref, cols) * dir_ref[rows, cols]
        image[:, 0:count] = value
        square[0, rows, :] = folded(value * res_ref[rows, cols])
        square[1, rows, :] = folded(value * value)

    for y in range(4):
        pl.when(lax.rem(plane, 4) == y)(lambda y=y: finish(y))
    first = jnp.where(lax.axis_index("coef") == 0, 1.0, 0.0)
    tile = tile_ref[...] + tile_of(
        [
            jnp.zeros((1, MEM), F32),
            first * member_row(curve_ref[...]),
            member_row(square[0]),
            member_row(square[1]),
        ]
    )
    for k in range(16):
        out_ref[k, :, 0:WIDE] = image[...]
        out_ref[k, :, WIDE:] = tile


def plane_sum_kernel(whole_ref, out_ref):
    tile = whole_ref[0]
    for k in range(1, 16):
        tile = tile + whole_ref[k]
    for k in range(16):
        out_ref[k] = tile


def update_kernel(
    own_ref, got_ref, sums_ref, sol_ref, res_ref, dir_ref, cimage_ref, csol_ref, cres_ref, cdir_ref,
    sol_hbm, res_hbm, dir_hbm, csol_hbm, cres_hbm, cdir_hbm,
    sol_buf, res_buf, dir_buf, csol_buf, cres_buf, cdir_buf, step_col, ratio_col, core_sems, sems,
):
    core = lax.axis_index("core")
    tile = sums_ref[0]
    for k in range(1, 16):
        tile = tile + sums_ref[k]
    tile = tile[:, 0:MEM]
    before = tile[0:1]
    step = before / tile[1:2]
    ratio = (before + step * (step * tile[3:4] - 2.0 * tile[2:3])) / before
    blank = jnp.zeros((1, 128 - MEM), F32)
    step_col[...] = turned(jnp.concatenate([step, blank], axis=1))
    ratio_col[...] = turned(jnp.concatenate([ratio, blank], axis=1))
    waits = []
    for y in range(4):
        cols = columns_of(y)
        count = (cols.stop - cols.start) // SEG
        for k in range(8):
            ref, part = (own_ref, core) if k < 4 else (got_ref, 1 - core)
            rows = pl.ds(pl.multiple_of(part * 32 + (k % 4) * 8, 8), 8)
            scale = jnp.concatenate([step_col[rows, :]] * count, axis=1)
            other = jnp.concatenate([ratio_col[rows, :]] * count, axis=1)
            direction = dir_ref[rows, cols]
            sol_buf[rows, cols] = sol_ref[rows, cols] + scale * direction
            new_res = res_ref[rows, cols] - scale * ref[k % 4, y, :, 0 : count * SEG]
            res_buf[rows, cols] = new_res
            dir_buf[rows, cols] = new_res + other * direction
        waits += out_copies(
            [
                (buf.at[:, cols], hbm.at[:, cols])
                for buf, hbm in ((sol_buf, sol_hbm), (res_buf, res_hbm), (dir_buf, dir_hbm))
            ],
            sems.at[y],
        )
    for j in range(NJ):
        csol_buf[j] = csol_ref[j] + step * cdir_ref[j]
        new_res = cres_ref[j] - step * cimage_ref[j]
        cres_buf[j] = new_res
        cdir_buf[j] = new_res + ratio * cdir_ref[j]
    waits += out_copies(
        [(csol_buf, csol_hbm), (cres_buf, cres_hbm), (cdir_buf, cdir_hbm)], core_sems
    )
    for copy in waits:
        copy.wait()


def shards(
    design_lith, design_core, sample_phase, data_weight, counts, knot_index, lith_damping, core_damping,
    lith_solution, lith_residual, lith_direction, core_solution, core_residual, core_direction,
):
    segments = ("plane", "core")
    tm = lax.axis_size("plane") * 2
    swap = [(0, 1), (1, 0)]
    csol, cres, cdir = (
        jnp.transpose(v, (1, 2, 0)) for v in (core_solution, core_residual, core_direction)
    )
    phase = sample_phase.reshape(8, SEG)
    weight = data_weight.reshape(8, SEG)
    damp = lith_damping.reshape(NL // SEG, SEG)
    upper = lax.ppermute(cdir, segments, [(t, (t - 1) % tm) for t in range(tm)])
    product_cost = pl.CostEstimate(
        flops=16 * MEM * NL * NS, bytes_accessed=12 * MIB, transcendentals=0
    )

    pin = lambda v: pltpu.with_memory_space_constraint(v, pltpu.HBM)
    lith, design, ghi, glo = pl.pallas_call(
        forward_kernel,
        out_shape=(
            struct((MEM, NS)),
            pltpu.VMEM((NL, NS), BF16),
            struct((JP * 16, NS), BF16),
            struct((JP * 16, NS), BF16),
        ),
        in_specs=[HB] * 5,
        out_specs=(VM,) * 4,
        scratch_shapes=[
            pltpu.VMEM((MEM, NL), F32),
            pltpu.VMEM((2 * MEM, NL), BF16),
            pltpu.VMEM((2 * MEM, NS), F32),
            pltpu.VMEM((NJ, NS), BF16),
            pltpu.VMEM((8, SEG), F32),
            pltpu.SMEM((8,), jnp.int32),
            pltpu.VMEM((16, NS), F32),
            pltpu.VMEM((JP, NS), F32),
            pltpu.SemaphoreType.DMA((4,)),
            pltpu.SemaphoreType.DMA((len(FORWARD_CUTS) - 1,)),
        ],
        compiler_params=params(24),
        cost_estimate=product_cost,
        name="forward",
    )(pin(lith_direction), pin(design_lith), pin(design_core), pin(phase), pin(knot_index))

    partial = pl.pallas_call(
        core_forward_kernel,
        out_shape=struct((8, 8, NS)),
        in_specs=[VM] * 5,
        out_specs=VM,
        scratch_shapes=[pltpu.VMEM((JP, 16, MEM), F32)],
        compiler_params=params(12),
        name="core_forward",
    )(lith, cdir, upper, ghi, glo)

    parts = lax.all_to_all(partial, "coef", 0, 0)
    total = pl.pallas_call(
        sum_kernel,
        out_shape=struct(parts.shape),
        in_specs=[VM],
        out_specs=VM,
        compiler_params=params(8),
        name="field_sum",
    )(parts)
    field = lax.all_to_all(total, "coef", 0, 0)

    pair, local, halo, curve = pl.pallas_call(
        core_back_kernel,
        out_shape=(
            struct((2 * MEM, NS), BF16),
            struct((NJ, 8, MEM)),
            struct((JP // 2, 8, 2 * MEM)),
            struct((MEM, SEG)),
        ),
        in_specs=[VM] * 4 + [SM],
        out_specs=(VM,) * 4,
        compiler_params=params(16),
        name="core_back",
    )(field, weight, ghi, glo, counts)
    lower = lax.ppermute(halo, segments, [(t, (t + 1) % tm) for t in range(tm)])

    chunks = struct((4, 4, 8, WIDE))
    core_struct = struct((NJ, 8, MEM))
    own, other = pl.pallas_call(
        back_kernel,
        out_shape=(chunks, chunks),
        in_specs=[VM, VM],
        out_specs=(VM, VM),
        scratch_shapes=[pltpu.VMEM((2 * MEM, NS), BF16)],
        compiler_params=params(12),
        cost_estimate=product_cost,
        name="back",
    )(pair, design)
    got = lax.ppermute(other, "core", swap)
    known = pl.pallas_call(
        known_sums_kernel,
        out_shape=struct((8, 128)),
        in_specs=[VM] * 5 + [SM],
        out_specs=VM,
        compiler_params=params(8),
        name="known_sums",
    )(cdir, cres, lith_direction, lith_residual, damp, core_damping)

    terms, known, cimage = pl.pallas_call(
        add_kernel,
        out_shape=(chunks, struct((8, 128)), core_struct),
        in_specs=[VM] * 7 + [SM],
        out_specs=(VM,) * 3,
        compiler_params=params(8),
        name="add_halves",
    )(own, got, known, local, lower, cdir, cres, core_damping)

    pieces = lax.all_to_all(terms.reshape(16, 8, WIDE), "plane", 0, 0)
    sent = pl.pallas_call(
        image_kernel,
        out_shape=struct((16, 8, SENT)),
        in_specs=[VM] * 6,
        out_specs=VM,
        scratch_shapes=[pltpu.VMEM((8, WIDE), F32), pltpu.VMEM((2, MEM, 128), F32)],
        compiler_params=params(12),
        name="image",
    )(pieces, curve, lith_direction, lith_residual, damp, known)
    whole = lax.all_to_all(sent, "plane", 0, 0)
    rest = lax.ppermute(whole, "core", swap).reshape(4, 4, 8, SENT)
    sums = pl.pallas_call(
        plane_sum_kernel,
        grid=(1,),
        out_shape=struct((16, 8, 128)),
        in_specs=[pl.BlockSpec((16, 8, 128), lambda i: (0, 0, WIDE // 128))],
        out_specs=pl.BlockSpec((16, 8, 128), lambda i: (0, 0, 0)),
        compiler_params=params(8),
        name="plane_sum",
    )(whole)
    sums = lax.all_to_all(sums, ("core", "coef"), 0, 0)
    whole = whole.reshape(4, 4, 8, SENT)

    lith_struct = struct((MEM, NL))
    new_sol, new_res, new_dir, new_csol, new_cres, new_cdir = pl.pallas_call(
        update_kernel,
        out_shape=(lith_struct,) * 3 + (core_struct,) * 3,
        in_specs=[VM] * 10,
        out_specs=(HB,) * 6,
        scratch_shapes=[pltpu.VMEM((MEM, NL), F32)] * 3
        + [pltpu.VMEM((NJ, 8, MEM), F32)] * 3
        + [pltpu.VMEM((128, 128), F32)] * 2
        + [pltpu.SemaphoreType.DMA((3,)), pltpu.SemaphoreType.DMA((4, 3))],
        compiler_params=params(20),
        name="update",
    )(
        whole, rest, sums, lith_solution, lith_residual, lith_direction, cimage, csol, cres, cdir,
    )
    back = lambda v: jnp.transpose(v, (2, 0, 1))
    return new_sol, new_res, new_dir, back(new_csol), back(new_cres), back(new_cdir)


def solution(mesh):
    parts = jax.sharding.Mesh(mesh.devices.reshape(-1, 2, mesh.devices.shape[1]), ("plane", "core", "coef"))
    segments = ("plane", "core")
    lith, core = P(None, "coef"), P(None, "coef", segments)
    return jax.shard_map(
        shards,
        mesh=parts,
        in_specs=(
            P("coef", segments), P("coef", segments), P(segments), P(segments), P(segments), P(segments),
            P("coef"), P("coef"), lith, lith, lith, core, core, core,
        ),
        out_specs=(lith, lith, lith, core, core, core),
        check_vma=False,
    )
```

```python
import jax
import jax.numpy as jnp
from jax import lax
from jax.experimental import pallas as pl
from jax.experimental.pallas import tpu as pltpu
from jax.sharding import PartitionSpec as P

NL, NS, MEM, NJ, JP = 4352, 1024, 64, 55, 56
GROWS = JP * 8
SEG = 128
WIDE, FULL, HALF, HALO = 1152, 1024, 64, 144
MIB = 1 << 20
F32, BF16 = jnp.float32, jnp.bfloat16
VM = pl.BlockSpec(memory_space=pltpu.VMEM)
SM = pl.BlockSpec(memory_space=pltpu.SMEM)
HB = pl.BlockSpec(memory_space=pltpu.HBM)
FORWARD_CUTS = (0, 512, 1280, 2304, 3328, 4352)
TRANS_B = (((1,), (1,)), ((), ()))


def params(mib):
    return pltpu.CompilerParams(vmem_limit_bytes=mib * MIB)


def struct(shape, dtype=F32):
    return jax.ShapeDtypeStruct(shape, dtype)


def split(values):
    high = values.astype(BF16)
    return high, (values - high.astype(F32)).astype(BF16)


def spline_values(u):
    now = [jnp.ones_like(u)]
    for d in range(1, 6):
        later = []
        for s in range(d + 1):
            term = 0.0
            if s >= 1:
                term = (u + float(d - s)) * now[s - 1]
            if s < d:
                term = term + (float(s + 1) - u) * now[s]
            later.append(term * (1.0 / d))
        now = later
    return now


def core_product(ext, ghi_ref, glo_ref, first):
    high, low = split(jnp.transpose(ext[...].reshape(GROWS, MEM)))
    both = jnp.concatenate([high, low], axis=0)
    rows = slice(first, first + GROWS)
    wide = jnp.dot(both, ghi_ref[rows, :], preferred_element_type=F32)
    low = jnp.dot(high, glo_ref[rows, :], preferred_element_type=F32)
    return wide[0:MEM] + wide[MEM:] + low


def forward_kernel(
    dir_hbm, a_hbm, design_hbm, phase_hbm, knot_hbm, cdir_hbm, out_ref, a_buf, ghi_ref, glo_ref,
    dir_buf, lhs, acc, design_buf, phase_buf, knot_buf, ext, basis, design, small_sems, sems,
):
    small = [
        pltpu.make_async_copy(src, dst, small_sems.at[k])
        for k, (src, dst) in enumerate(
            (
                (phase_hbm, phase_buf), (knot_hbm, knot_buf), (design_hbm, design_buf),
                (cdir_hbm, ext.at[0:NJ]), (dir_hbm, dir_buf),
            )
        )
    ]
    for copy in small:
        copy.start()
    copies = []
    for b in range(len(FORWARD_CUTS) - 1):
        rows = pl.ds(FORWARD_CUTS[b], FORWARD_CUTS[b + 1] - FORWARD_CUTS[b])
        copy = pltpu.make_async_copy(a_hbm.at[rows], a_buf.at[rows], sems.at[b])
        copy.start()
        copies.append(copy)
    for copy in small[0:4]:
        copy.wait()
    values = spline_values(phase_buf[...])
    row = lax.broadcasted_iota(jnp.int32, (16, SEG), 0)
    for g in range(8):
        first = lax.rem(knot_buf[g], 8)
        block = jnp.zeros((16, SEG), F32)
        for k in range(6):
            block = block + jnp.where(row == first + k, values[k][g : g + 1, :], 0.0)
        basis[:, g * SEG : (g + 1) * SEG] = block
    design[0:NJ] = design_buf[...].astype(F32)
    design[NJ:JP] = jnp.zeros((1, NS), F32)

    def build(j, carry):
        for part in range(2):
            spline = basis[part * 8 : part * 8 + 8, :]
            product = jnp.concatenate(
                [spline * design[pl.ds(2 * j + k, 1), :] for k in range(2)], axis=0
            )
            high, low = split(product)
            rows = pl.ds(pl.multiple_of(part * GROWS + j * 16, 16), 16)
            ghi_ref[rows, :] = high
            glo_ref[rows, :] = low
        return carry

    lax.fori_loop(0, JP // 2, build, 0)
    ext[NJ:JP] = jnp.zeros((1, 8, MEM), F32)
    out_ref[...] = core_product(ext, ghi_ref, glo_ref, 0)
    small[4].wait()
    for b, copy in enumerate(copies):
        lo, hi = FORWARD_CUTS[b], FORWARD_CUTS[b + 1]
        high, low = split(dir_buf[:, lo:hi])
        lhs[0:MEM, lo:hi] = high
        lhs[MEM:, lo:hi] = low
        copy.wait()
        part = jnp.dot(lhs[:, lo:hi], a_buf[lo:hi], preferred_element_type=F32)
        if b == 0:
            acc[...] = part
        else:
            acc[...] += part
    out_ref[...] += acc[0:MEM] + acc[MEM:]


def core_forward_kernel(lith_ref, halo_ref, ghi_ref, glo_ref, out_ref, ext):
    last = jnp.logical_and(lax.axis_index("plane") == 15, lax.axis_index("core") == 1)
    ext[0:NJ] = halo_ref[...] * jnp.where(last, 0.0, 1.0)
    ext[NJ:JP] = jnp.zeros((1, 8, MEM), F32)
    value = core_product(ext, ghi_ref, glo_ref, GROWS) + lith_ref[...]
    out_ref[...] = value.reshape(8, 8, NS)


def sum_kernel(parts_ref, out_ref):
    total = parts_ref[0]
    for k in range(1, parts_ref.shape[0]):
        total = total + parts_ref[k]
    for k in range(parts_ref.shape[0]):
        out_ref[k] = total


def back_kernel(
    field_ref, weight_ref, ghi_ref, glo_ref, a_ref, count_ref,
    own_ref, other_ref, local_ref, halo_ref, curve_ref, pair, lhs,
):
    lane = lax.broadcasted_iota(jnp.int32, (1, SEG), 1)
    curve = jnp.zeros((MEM, SEG), F32)
    for g in range(8):
        cols = slice(g * SEG, (g + 1) * SEG)
        weight = jnp.where(lane < count_ref[g], weight_ref[g : g + 1, :], 0.0)
        field = field_ref[:, :, cols].reshape(MEM, SEG)
        residual = field * weight
        curve = curve + residual * field
        high, low = split(residual)
        pair[0:MEM, cols] = high
        pair[MEM:, cols] = low
    curve_ref[...] = curve
    half = MEM // 2
    core = lax.axis_index("core")
    mine = pl.multiple_of(core * half, half)
    theirs = pl.multiple_of((1 - core) * half, half)
    for k, start in enumerate((mine, theirs, MEM + mine, MEM + theirs)):
        lhs[k * half : (k + 1) * half] = pair[pl.ds(pl.multiple_of(start, half), half), :]

    def product(rows):
        part = lax.dot_general(lhs[...], a_ref[rows], TRANS_B, preferred_element_type=F32)
        part = part[0:MEM] + part[MEM:]
        return part[0:half], part[half:]

    for y in range(4):
        for out, part in zip((own_ref, other_ref), product(slice(y * FULL, (y + 1) * FULL))):
            out[:, y, :, 0:FULL] = part.reshape(4, 8, FULL)
    for out, part in zip((own_ref, other_ref), product(slice(4 * FULL, NL))):
        for y in range(4):
            tail = part[:, y // 2 * SEG : (y // 2 + 1) * SEG]
            out[:, y, :, FULL:] = tail.reshape(4, 8, SEG)
    wide = lax.dot_general(ghi_ref[...], pair[...], TRANS_B, preferred_element_type=F32)
    low = lax.dot_general(glo_ref[...], pair[0:MEM], TRANS_B, preferred_element_type=F32)
    grad = (wide[:, 0:MEM] + wide[:, MEM:] + low).reshape(2, JP, 8, MEM)
    local_ref[...] = grad[0, 0:NJ]
    packed = jnp.concatenate([grad[1, 0 : JP // 2], grad[1, JP // 2 :]], axis=2)
    for j in range(JP // 2):
        halo_ref[j * 5 : j * 5 + 5, :] = packed[j, 0:5, :]
    halo_ref[JP // 2 * 5 :, :] = jnp.zeros((HALO - JP // 2 * 5, 128), F32)


def add_kernel(
    own_ref, got_ref, tile_ref, local_ref, halo_ref, cdir_ref, cres_ref, cdamp_ref,
    out_ref, tile_out_ref, cimage_ref,
):
    out_ref[...] = own_ref[...] + got_ref[...]
    cross = jnp.zeros((8, MEM), F32)
    norm = jnp.zeros((8, MEM), F32)
    first = jnp.logical_and(lax.axis_index("plane") == 0, lax.axis_index("core") == 0)
    row = lax.broadcasted_iota(jnp.int32, (8, 128), 0)
    inside = jnp.where(row < 5, jnp.where(first, 0.0, 1.0), 0.0)
    for j in range(NJ):
        place = j % (JP // 2) * 5
        packed = halo_ref[place : place + 8, :] * inside
        halo = packed[:, 0:MEM] if j < JP // 2 else packed[:, MEM:]
        core_image = local_ref[j] + halo + cdamp_ref[j] * cdir_ref[j]
        cimage_ref[j] = core_image
        cross = cross + cres_ref[j] * core_image
        norm = norm + core_image * core_image
    zero = jnp.zeros((1, MEM), F32)
    tile_out_ref[...] = tile_ref[...] + tile_of(
        [zero, zero, jnp.sum(cross, axis=0, keepdims=True), jnp.sum(norm, axis=0, keepdims=True)]
    )


def turned(row):
    return jnp.transpose(jnp.broadcast_to(row, (128, 128)))


def out_copies(pairs, sems):
    copies = [
        pltpu.make_async_copy(src, dst, sems.at[k]) for k, (src, dst) in enumerate(pairs)
    ]
    for copy in copies:
        copy.start()
    return copies


def damp_rows(damp_ref, cols):
    rows = range(cols.start // SEG, cols.stop // SEG)
    return jnp.concatenate(
        [jnp.broadcast_to(damp_ref[t : t + 1, :], (8, SEG)) for t in rows], axis=1
    )


def folded(values):
    total = values[:, 0:SEG]
    for t in range(1, values.shape[1] // SEG):
        total = total + values[:, t * SEG : (t + 1) * SEG]
    return total


def member_row(columns):
    padded = jnp.concatenate([columns, jnp.zeros((128 - MEM, 128), F32)], axis=0)
    return jnp.sum(jnp.transpose(padded), axis=0, keepdims=True)[:, 0:MEM]


def tile_of(rows):
    tile = jnp.concatenate(rows + [jnp.zeros((8 - len(rows), MEM), F32)], axis=0)
    return jnp.concatenate([tile, jnp.zeros((8, 128 - MEM), F32)], axis=1)


def known_sums_kernel(cdir_ref, cres_ref, dir_ref, res_ref, damp_ref, cdamp_ref, tile_ref):
    before = jnp.zeros((8, MEM), F32)
    curve = jnp.zeros((8, MEM), F32)
    for j in range(NJ):
        before = before + cres_ref[j] * cres_ref[j]
        curve = curve + cdamp_ref[j] * (cdir_ref[j] * cdir_ref[j])
    lith_before = jnp.zeros((MEM, SEG), F32)
    lith_curve = jnp.zeros((MEM, SEG), F32)
    for t in range(NL // SEG):
        cols = slice(t * SEG, (t + 1) * SEG)
        lith_before = lith_before + res_ref[:, cols] * res_ref[:, cols]
        lith_curve = lith_curve + dir_ref[:, cols] * dir_ref[:, cols] * damp_ref[t : t + 1, :]
    once = jnp.logical_and(lax.axis_index("plane") == 0, lax.axis_index("core") == 0)
    once = jnp.where(once, 1.0, 0.0)
    tile_ref[...] = tile_of(
        [
            jnp.sum(c, axis=0, keepdims=True) + once * member_row(v)
            for c, v in ((before, lith_before), (curve, lith_curve))
        ]
    )


def image_kernel(parts_ref, curve_ref, dir_ref, res_ref, damp_ref, tile_ref, out_ref, image, square):
    total = parts_ref[0]
    for k in range(1, 16):
        total = total + parts_ref[k]
    image[...] = total
    square[...] = jnp.zeros((2, MEM, 128), F32)
    plane = lax.axis_index("plane")
    rows = pl.ds(pl.multiple_of((lax.axis_index("core") * 4 + plane // 4) * 8, 8), 8)
    lane = lax.broadcasted_iota(jnp.int32, (8, SEG), 1)
    mine = lane // HALF == lax.rem(plane, 2)

    def finish(y):
        cols = slice(y * FULL, (y + 1) * FULL)
        tail = slice(4 * FULL + y // 2 * SEG, 4 * FULL + (y // 2 + 1) * SEG)
        value = image[:, 0:FULL] + damp_rows(damp_ref, cols) * dir_ref[rows, cols]
        rest = image[:, FULL:] + damp_rows(damp_ref, tail) * dir_ref[rows, tail]
        rest = jnp.where(mine, rest, 0.0)
        image[:, 0:FULL] = value
        image[:, FULL:] = rest
        square[0, rows, :] = folded(value * res_ref[rows, cols]) + rest * res_ref[rows, tail]
        square[1, rows, :] = folded(value * value) + rest * rest

    for y in range(4):
        pl.when(lax.rem(plane, 4) == y)(lambda y=y: finish(y))
    first = jnp.where(lax.axis_index("coef") == 0, 1.0, 0.0)
    tile = tile_ref[...] + tile_of(
        [
            jnp.zeros((1, MEM), F32),
            first * member_row(curve_ref[...]),
            member_row(square[0]),
            member_row(square[1]),
        ]
    )
    tile = jnp.concatenate([tile[:, 0:HALF], tile[:, 0:HALF]], axis=1)
    rest = jnp.where(mine, image[:, FULL:], tile)
    for k in range(16):
        out_ref[k, :, 0:FULL] = image[:, 0:FULL]
        out_ref[k, :, FULL:] = rest


def plane_sum_kernel(whole_ref, out_ref):
    even, odd = whole_ref[0], whole_ref[1]
    for k in range(2, 16, 2):
        even = even + whole_ref[k]
        odd = odd + whole_ref[k + 1]
    tile = odd[:, 0:HALF] + even[:, HALF:]
    tile = jnp.concatenate([tile, jnp.zeros((8, SEG - HALF), F32)], axis=1)
    for k in range(16):
        out_ref[k] = tile


def update_kernel(
    own_ref, got_ref, sums_ref, sol_ref, res_ref, dir_ref, cimage_ref, csol_ref, cres_ref, cdir_ref,
    sol_hbm, res_hbm, dir_hbm, csol_hbm, cres_hbm, cdir_hbm,
    sol_buf, res_buf, dir_buf, csol_buf, cres_buf, cdir_buf, step_col, ratio_col, core_sems, sems,
):
    core = lax.axis_index("core")
    tile = sums_ref[0]
    for k in range(1, 16):
        tile = tile + sums_ref[k]
    tile = tile[:, 0:MEM]
    before = tile[0:1]
    step = before / tile[1:2]
    ratio = (before + step * (step * tile[3:4] - 2.0 * tile[2:3])) / before
    for j in range(NJ):
        csol_buf[j] = csol_ref[j] + step * cdir_ref[j]
        new_res = cres_ref[j] - step * cimage_ref[j]
        cres_buf[j] = new_res
        cdir_buf[j] = new_res + ratio * cdir_ref[j]
    waits = out_copies(
        [(csol_buf, csol_hbm), (cres_buf, cres_hbm), (cdir_buf, cdir_hbm)], core_sems
    )
    blank = jnp.zeros((1, 128 - MEM), F32)
    step_col[...] = turned(jnp.concatenate([step, blank], axis=1))
    ratio_col[...] = turned(jnp.concatenate([ratio, blank], axis=1))
    lane = lax.broadcasted_iota(jnp.int32, (8, SEG), 1)
    for y in range(5):
        cols = slice(y * FULL, min((y + 1) * FULL, NL))
        count = (cols.stop - cols.start) // SEG
        for k in range(8):
            ref, part = (own_ref, core) if k < 4 else (got_ref, 1 - core)
            rows = pl.ds(pl.multiple_of(part * 32 + (k % 4) * 8, 8), 8)
            if y < 4:
                image = ref[k % 4, y, :, 0:FULL]
            else:
                tails = [ref[k % 4, t, :, FULL:] for t in range(4)]
                image = jnp.concatenate(
                    [jnp.where(lane < HALF, tails[t], tails[t + 1]) for t in (0, 2)], axis=1
                )
            scale = jnp.concatenate([step_col[rows, :]] * count, axis=1)
            other = jnp.concatenate([ratio_col[rows, :]] * count, axis=1)
            direction = dir_ref[rows, cols]
            sol_buf[rows, cols] = sol_ref[rows, cols] + scale * direction
            new_res = res_ref[rows, cols] - scale * image
            res_buf[rows, cols] = new_res
            dir_buf[rows, cols] = new_res + other * direction
        waits += out_copies(
            [
                (buf.at[:, cols], hbm.at[:, cols])
                for buf, hbm in ((sol_buf, sol_hbm), (res_buf, res_hbm), (dir_buf, dir_hbm))
            ],
            sems.at[y],
        )
    for copy in waits:
        copy.wait()


def shards(
    design_lith, design_core, sample_phase, data_weight, counts, knot_index, lith_damping, core_damping,
    lith_solution, lith_residual, lith_direction, core_solution, core_residual, core_direction,
):
    segments = ("plane", "core")
    tm = lax.axis_size("plane") * 2
    swap = [(0, 1), (1, 0)]
    csol, cres, cdir = (
        jnp.transpose(v, (1, 2, 0)) for v in (core_solution, core_residual, core_direction)
    )
    phase = sample_phase.reshape(8, SEG)
    weight = data_weight.reshape(8, SEG)
    damp = lith_damping.reshape(NL // SEG, SEG)
    upper = lax.ppermute(cdir, segments, [(t, (t - 1) % tm) for t in range(tm)])
    product_cost = pl.CostEstimate(
        flops=16 * MEM * NL * NS, bytes_accessed=12 * MIB, transcendentals=0
    )

    pin = lambda v: pltpu.with_memory_space_constraint(v, pltpu.HBM)
    lith, design, ghi, glo = pl.pallas_call(
        forward_kernel,
        out_shape=(
            struct((MEM, NS)),
            pltpu.VMEM((NL, NS), BF16),
            struct((JP * 16, NS), BF16),
            struct((JP * 16, NS), BF16),
        ),
        in_specs=[HB] * 6,
        out_specs=(VM,) * 4,
        scratch_shapes=[
            pltpu.VMEM((MEM, NL), F32),
            pltpu.VMEM((2 * MEM, NL), BF16),
            pltpu.VMEM((2 * MEM, NS), F32),
            pltpu.VMEM((NJ, NS), BF16),
            pltpu.VMEM((8, SEG), F32),
            pltpu.SMEM((8,), jnp.int32),
            pltpu.VMEM((JP, 8, MEM), F32),
            pltpu.VMEM((16, NS), F32),
            pltpu.VMEM((JP, NS), F32),
            pltpu.SemaphoreType.DMA((5,)),
            pltpu.SemaphoreType.DMA((len(FORWARD_CUTS) - 1,)),
        ],
        compiler_params=params(24),
        cost_estimate=product_cost,
        name="forward",
    )(pin(lith_direction), pin(design_lith), pin(design_core), pin(phase), pin(knot_index), pin(cdir))

    partial = pl.pallas_call(
        core_forward_kernel,
        out_shape=struct((8, 8, NS)),
        in_specs=[VM] * 4,
        out_specs=VM,
        scratch_shapes=[pltpu.VMEM((JP, 8, MEM), F32)],
        compiler_params=params(12),
        name="core_forward",
    )(lith, upper, ghi, glo)

    parts = lax.all_to_all(partial, "coef", 0, 0)
    total = pl.pallas_call(
        sum_kernel,
        out_shape=struct(parts.shape),
        in_specs=[VM],
        out_specs=VM,
        compiler_params=params(8),
        name="field_sum",
    )(parts)
    field = lax.all_to_all(total, "coef", 0, 0)

    chunks = struct((4, 4, 8, WIDE))
    core_struct = struct((NJ, 8, MEM))
    own, other, local, halo, curve = pl.pallas_call(
        back_kernel,
        out_shape=(chunks, chunks, core_struct, struct((HALO, 128)), struct((MEM, SEG))),
        in_specs=[VM] * 5 + [SM],
        out_specs=(VM,) * 5,
        scratch_shapes=[pltpu.VMEM((2 * MEM, NS), BF16), pltpu.VMEM((2 * MEM, NS), BF16)],
        compiler_params=params(16),
        cost_estimate=product_cost,
        name="back",
    )(field, weight, ghi, glo, design, counts)
    lower = lax.ppermute(halo, segments, [(t, (t + 1) % tm) for t in range(tm)])
    got = lax.ppermute(other, "core", swap)
    known = pl.pallas_call(
        known_sums_kernel,
        out_shape=struct((8, 128)),
        in_specs=[VM] * 5 + [SM],
        out_specs=VM,
        compiler_params=params(8),
        name="known_sums",
    )(cdir, cres, lith_direction, lith_residual, damp, core_damping)

    terms, known, cimage = pl.pallas_call(
        add_kernel,
        out_shape=(chunks, struct((8, 128)), core_struct),
        in_specs=[VM] * 7 + [SM],
        out_specs=(VM,) * 3,
        compiler_params=params(8),
        name="add_halves",
    )(own, got, known, local, lower, cdir, cres, core_damping)

    pieces = lax.all_to_all(terms.reshape(16, 8, WIDE), "plane", 0, 0)
    sent = pl.pallas_call(
        image_kernel,
        out_shape=struct((16, 8, WIDE)),
        in_specs=[VM] * 6,
        out_specs=VM,
        scratch_shapes=[pltpu.VMEM((8, WIDE), F32), pltpu.VMEM((2, MEM, 128), F32)],
        compiler_params=params(12),
        name="image",
    )(pieces, curve, lith_direction, lith_residual, damp, known)
    whole = lax.all_to_all(sent, "plane", 0, 0)
    rest = lax.ppermute(whole, "core", swap).reshape(4, 4, 8, WIDE)
    sums = pl.pallas_call(
        plane_sum_kernel,
        grid=(1,),
        out_shape=struct((16, 8, 128)),
        in_specs=[pl.BlockSpec((16, 8, 128), lambda i: (0, 0, FULL // 128))],
        out_specs=pl.BlockSpec((16, 8, 128), lambda i: (0, 0, 0)),
        compiler_params=params(8),
        name="plane_sum",
    )(whole)
    sums = lax.all_to_all(sums, ("core", "coef"), 0, 0)
    whole = whole.reshape(4, 4, 8, WIDE)

    lith_struct = struct((MEM, NL))
    new_sol, new_res, new_dir, new_csol, new_cres, new_cdir = pl.pallas_call(
        update_kernel,
        out_shape=(lith_struct,) * 3 + (core_struct,) * 3,
        in_specs=[VM] * 10,
        out_specs=(HB,) * 6,
        scratch_shapes=[pltpu.VMEM((MEM, NL), F32)] * 3
        + [pltpu.VMEM((NJ, 8, MEM), F32)] * 3
        + [pltpu.VMEM((128, 128), F32)] * 2
        + [pltpu.SemaphoreType.DMA((3,)), pltpu.SemaphoreType.DMA((5, 3))],
        compiler_params=params(20),
        name="update",
    )(
        whole, rest, sums, lith_solution, lith_residual, lith_direction, cimage, csol, cres, cdir,
    )
    first = lambda v: jnp.transpose(v, (2, 0, 1))
    return new_sol, new_res, new_dir, first(new_csol), first(new_cres), first(new_cdir)


def solution(mesh):
    parts = jax.sharding.Mesh(mesh.devices.reshape(-1, 2, mesh.devices.shape[1]), ("plane", "core", "coef"))
    segments = ("plane", "core")
    lith, core = P(None, "coef"), P(None, "coef", segments)
    return jax.shard_map(
        shards,
        mesh=parts,
        in_specs=(
            P("coef", segments), P("coef", segments), P(segments), P(segments), P(segments), P(segments),
            P("coef"), P("coef"), lith, lith, lith, core, core, core,
        ),
        out_specs=(lith, lith, lith, core, core, core),
        check_vma=False,
    )
```

```python
import jax
import jax.numpy as jnp
from jax import lax
from jax.experimental import pallas as pl
from jax.experimental.pallas import tpu as pltpu
from jax.sharding import PartitionSpec as P

NL, NS, MEM, NJ, JP = 4352, 1024, 64, 55, 56
GROWS = JP * 8
SEG = 128
WIDE, FULL, HALF, HALO = 1152, 1024, 64, 144
MIB = 1 << 20
F32, BF16 = jnp.float32, jnp.bfloat16
VM = pl.BlockSpec(memory_space=pltpu.VMEM)
SM = pl.BlockSpec(memory_space=pltpu.SMEM)
HB = pl.BlockSpec(memory_space=pltpu.HBM)
FORWARD_CUTS = (0, 512, 1280, 2304, 3328, 4352)
TRANS_B = (((1,), (1,)), ((), ()))


def params(mib):
    return pltpu.CompilerParams(vmem_limit_bytes=mib * MIB)


def struct(shape, dtype=F32):
    return jax.ShapeDtypeStruct(shape, dtype)


def split(values):
    high = values.astype(BF16)
    return high, (values - high.astype(F32)).astype(BF16)


def spline_values(u):
    now = [jnp.ones_like(u)]
    for d in range(1, 6):
        later = []
        for s in range(d + 1):
            term = 0.0
            if s >= 1:
                term = (u + float(d - s)) * now[s - 1]
            if s < d:
                term = term + (float(s + 1) - u) * now[s]
            later.append(term * (1.0 / d))
        now = later
    return now


def core_product(ext, ghi_ref, glo_ref, first):
    high, low = split(jnp.transpose(ext[...].reshape(GROWS, MEM)))
    both = jnp.concatenate([high, low], axis=0)
    rows = slice(first, first + GROWS)
    wide = jnp.dot(both, ghi_ref[rows, :], preferred_element_type=F32)
    low = jnp.dot(high, glo_ref[rows, :], preferred_element_type=F32)
    return wide[0:MEM] + wide[MEM:] + low


def forward_kernel(
    dir_hbm, a_hbm, design_ref, phase_hbm, knot_hbm, cdir_hbm, out_ref, a_buf, ghi_ref, glo_ref,
    dir_buf, lhs, acc, phase_buf, knot_buf, ext, basis, design, small_sems, sems,
):
    small = [
        pltpu.make_async_copy(src, dst, small_sems.at[k])
        for k, (src, dst) in enumerate(
            (
                (phase_hbm, phase_buf), (knot_hbm, knot_buf),
                (cdir_hbm, ext.at[0:NJ]), (dir_hbm, dir_buf),
            )
        )
    ]
    for copy in small:
        copy.start()
    copies = []
    for b in range(len(FORWARD_CUTS) - 1):
        rows = pl.ds(FORWARD_CUTS[b], FORWARD_CUTS[b + 1] - FORWARD_CUTS[b])
        copy = pltpu.make_async_copy(a_hbm.at[rows], a_buf.at[rows], sems.at[b])
        copy.start()
        copies.append(copy)
    for copy in small[0:3]:
        copy.wait()
    values = spline_values(phase_buf[...])
    row = lax.broadcasted_iota(jnp.int32, (16, SEG), 0)
    for g in range(8):
        first = lax.rem(knot_buf[g], 8)
        block = jnp.zeros((16, SEG), F32)
        for k in range(6):
            block = block + jnp.where(row == first + k, values[k][g : g + 1, :], 0.0)
        basis[:, g * SEG : (g + 1) * SEG] = block
    design[0:NJ] = design_ref[...].astype(F32)
    design[NJ:JP] = jnp.zeros((1, NS), F32)

    def build(j, carry):
        for part in range(2):
            spline = basis[part * 8 : part * 8 + 8, :]
            product = jnp.concatenate(
                [spline * design[pl.ds(2 * j + k, 1), :] for k in range(2)], axis=0
            )
            high, low = split(product)
            rows = pl.ds(pl.multiple_of(part * GROWS + j * 16, 16), 16)
            ghi_ref[rows, :] = high
            glo_ref[rows, :] = low
        return carry

    lax.fori_loop(0, JP // 2, build, 0)
    ext[NJ:JP] = jnp.zeros((1, 8, MEM), F32)
    out_ref[...] = core_product(ext, ghi_ref, glo_ref, 0)
    small[3].wait()
    for b, copy in enumerate(copies):
        lo, hi = FORWARD_CUTS[b], FORWARD_CUTS[b + 1]
        high, low = split(dir_buf[:, lo:hi])
        lhs[0:MEM, lo:hi] = high
        lhs[MEM:, lo:hi] = low
        copy.wait()
        part = jnp.dot(lhs[:, lo:hi], a_buf[lo:hi], preferred_element_type=F32)
        if b == 0:
            acc[...] = part
        else:
            acc[...] += part
    out_ref[...] += acc[0:MEM] + acc[MEM:]


def core_forward_kernel(lith_ref, halo_ref, ghi_ref, glo_ref, out_ref, ext):
    last = jnp.logical_and(lax.axis_index("plane") == 15, lax.axis_index("core") == 1)
    ext[0:NJ] = halo_ref[...] * jnp.where(last, 0.0, 1.0)
    ext[NJ:JP] = jnp.zeros((1, 8, MEM), F32)
    value = core_product(ext, ghi_ref, glo_ref, GROWS) + lith_ref[...]
    out_ref[...] = value.reshape(8, 8, NS)


def sum_kernel(parts_ref, out_ref):
    total = parts_ref[0]
    for k in range(1, parts_ref.shape[0]):
        total = total + parts_ref[k]
    for k in range(parts_ref.shape[0]):
        out_ref[k] = total


def back_kernel(
    field_ref, weight_ref, ghi_ref, glo_ref, a_ref, count_ref,
    own_ref, other_ref, local_ref, halo_ref, curve_ref, pair, lhs,
):
    lane = lax.broadcasted_iota(jnp.int32, (1, SEG), 1)
    curve = jnp.zeros((MEM, SEG), F32)
    for g in range(8):
        cols = slice(g * SEG, (g + 1) * SEG)
        weight = jnp.where(lane < count_ref[g], weight_ref[g : g + 1, :], 0.0)
        field = field_ref[:, :, cols].reshape(MEM, SEG)
        residual = field * weight
        curve = curve + residual * field
        high, low = split(residual)
        pair[0:MEM, cols] = high
        pair[MEM:, cols] = low
    curve_ref[...] = curve
    half = MEM // 2
    core = lax.axis_index("core")
    mine = pl.multiple_of(core * half, half)
    theirs = pl.multiple_of((1 - core) * half, half)
    for k, start in enumerate((mine, theirs, MEM + mine, MEM + theirs)):
        lhs[k * half : (k + 1) * half] = pair[pl.ds(pl.multiple_of(start, half), half), :]

    def product(rows):
        part = lax.dot_general(lhs[...], a_ref[rows], TRANS_B, preferred_element_type=F32)
        part = part[0:MEM] + part[MEM:]
        return part[0:half], part[half:]

    for y in range(4):
        for out, part in zip((own_ref, other_ref), product(slice(y * FULL, (y + 1) * FULL))):
            out[:, y, :, 0:FULL] = part.reshape(4, 8, FULL)
    for out, part in zip((own_ref, other_ref), product(slice(4 * FULL, NL))):
        for y in range(4):
            tail = part[:, y // 2 * SEG : (y // 2 + 1) * SEG]
            out[:, y, :, FULL:] = tail.reshape(4, 8, SEG)
    wide = lax.dot_general(ghi_ref[...], pair[...], TRANS_B, preferred_element_type=F32)
    low = lax.dot_general(glo_ref[...], pair[0:MEM], TRANS_B, preferred_element_type=F32)
    grad = (wide[:, 0:MEM] + wide[:, MEM:] + low).reshape(2, JP, 8, MEM)
    local_ref[...] = grad[0, 0:NJ]
    packed = jnp.concatenate([grad[1, 0 : JP // 2], grad[1, JP // 2 :]], axis=2)
    for j in range(JP // 2):
        halo_ref[j * 5 : j * 5 + 5, :] = packed[j, 0:5, :]
    halo_ref[JP // 2 * 5 :, :] = jnp.zeros((HALO - JP // 2 * 5, 128), F32)


def add_kernel(
    own_ref, got_ref, tile_ref, local_ref, halo_ref, cdir_ref, cres_ref, cdamp_ref,
    out_ref, tile_out_ref, cimage_ref,
):
    out_ref[...] = own_ref[...] + got_ref[...]
    cross = jnp.zeros((8, MEM), F32)
    norm = jnp.zeros((8, MEM), F32)
    first = jnp.logical_and(lax.axis_index("plane") == 0, lax.axis_index("core") == 0)
    row = lax.broadcasted_iota(jnp.int32, (8, 128), 0)
    inside = jnp.where(row < 5, jnp.where(first, 0.0, 1.0), 0.0)
    for j in range(NJ):
        place = j % (JP // 2) * 5
        packed = halo_ref[place : place + 8, :] * inside
        halo = packed[:, 0:MEM] if j < JP // 2 else packed[:, MEM:]
        core_image = local_ref[j] + halo + cdamp_ref[j] * cdir_ref[j]
        cimage_ref[j] = core_image
        cross = cross + cres_ref[j] * core_image
        norm = norm + core_image * core_image
    zero = jnp.zeros((1, MEM), F32)
    tile_out_ref[...] = tile_ref[...] + tile_of(
        [zero, zero, jnp.sum(cross, axis=0, keepdims=True), jnp.sum(norm, axis=0, keepdims=True)]
    )


def turned(row):
    return jnp.transpose(jnp.broadcast_to(row, (128, 128)))


def out_copies(pairs, sems):
    copies = [
        pltpu.make_async_copy(src, dst, sems.at[k]) for k, (src, dst) in enumerate(pairs)
    ]
    for copy in copies:
        copy.start()
    return copies


def damp_rows(damp_ref, cols):
    rows = range(cols.start // SEG, cols.stop // SEG)
    return jnp.concatenate(
        [jnp.broadcast_to(damp_ref[t : t + 1, :], (8, SEG)) for t in rows], axis=1
    )


def folded(values):
    total = values[:, 0:SEG]
    for t in range(1, values.shape[1] // SEG):
        total = total + values[:, t * SEG : (t + 1) * SEG]
    return total


def member_row(columns):
    padded = jnp.concatenate([columns, jnp.zeros((128 - MEM, 128), F32)], axis=0)
    return jnp.sum(jnp.transpose(padded), axis=0, keepdims=True)[:, 0:MEM]


def tile_of(rows):
    tile = jnp.concatenate(rows + [jnp.zeros((8 - len(rows), MEM), F32)], axis=0)
    return jnp.concatenate([tile, jnp.zeros((8, 128 - MEM), F32)], axis=1)


def known_sums_kernel(cdir_ref, cres_ref, dir_ref, res_ref, damp_ref, cdamp_ref, tile_ref):
    before = jnp.zeros((8, MEM), F32)
    curve = jnp.zeros((8, MEM), F32)
    for j in range(NJ):
        before = before + cres_ref[j] * cres_ref[j]
        curve = curve + cdamp_ref[j] * (cdir_ref[j] * cdir_ref[j])
    lith_before = jnp.zeros((MEM, SEG), F32)
    lith_curve = jnp.zeros((MEM, SEG), F32)
    for t in range(NL // SEG):
        cols = slice(t * SEG, (t + 1) * SEG)
        lith_before = lith_before + res_ref[:, cols] * res_ref[:, cols]
        lith_curve = lith_curve + dir_ref[:, cols] * dir_ref[:, cols] * damp_ref[t : t + 1, :]
    once = jnp.logical_and(lax.axis_index("plane") == 0, lax.axis_index("core") == 0)
    once = jnp.where(once, 1.0, 0.0)
    tile_ref[...] = tile_of(
        [
            jnp.sum(c, axis=0, keepdims=True) + once * member_row(v)
            for c, v in ((before, lith_before), (curve, lith_curve))
        ]
    )


def image_kernel(parts_ref, curve_ref, dir_ref, res_ref, damp_ref, tile_ref, out_ref, image, square):
    total = parts_ref[0]
    for k in range(1, 16):
        total = total + parts_ref[k]
    image[...] = total
    square[...] = jnp.zeros((2, MEM, 128), F32)
    plane = lax.axis_index("plane")
    rows = pl.ds(pl.multiple_of((lax.axis_index("core") * 4 + plane // 4) * 8, 8), 8)
    lane = lax.broadcasted_iota(jnp.int32, (8, SEG), 1)
    mine = lane // HALF == lax.rem(plane, 2)

    def finish(y):
        cols = slice(y * FULL, (y + 1) * FULL)
        tail = slice(4 * FULL + y // 2 * SEG, 4 * FULL + (y // 2 + 1) * SEG)
        value = image[:, 0:FULL] + damp_rows(damp_ref, cols) * dir_ref[rows, cols]
        rest = image[:, FULL:] + damp_rows(damp_ref, tail) * dir_ref[rows, tail]
        rest = jnp.where(mine, rest, 0.0)
        image[:, 0:FULL] = value
        image[:, FULL:] = rest
        square[0, rows, :] = folded(value * res_ref[rows, cols]) + rest * res_ref[rows, tail]
        square[1, rows, :] = folded(value * value) + rest * rest

    for y in range(4):
        pl.when(lax.rem(plane, 4) == y)(lambda y=y: finish(y))
    first = jnp.where(lax.axis_index("coef") == 0, 1.0, 0.0)
    tile = tile_ref[...] + tile_of(
        [
            jnp.zeros((1, MEM), F32),
            first * member_row(curve_ref[...]),
            member_row(square[0]),
            member_row(square[1]),
        ]
    )
    tile = jnp.concatenate([tile[:, 0:HALF], tile[:, 0:HALF]], axis=1)
    rest = jnp.where(mine, image[:, FULL:], tile)
    for k in range(16):
        out_ref[k, :, 0:FULL] = image[:, 0:FULL]
        out_ref[k, :, FULL:] = rest


def plane_sum_kernel(whole_ref, out_ref):
    even, odd = whole_ref[0], whole_ref[1]
    for k in range(2, 16, 2):
        even = even + whole_ref[k]
        odd = odd + whole_ref[k + 1]
    tile = odd[:, 0:HALF] + even[:, HALF:]
    tile = jnp.concatenate([tile, jnp.zeros((8, SEG - HALF), F32)], axis=1)
    for k in range(16):
        out_ref[k] = tile


def update_kernel(
    own_ref, got_ref, sums_ref, sol_ref, res_ref, dir_ref, cimage_ref, csol_ref, cres_ref, cdir_ref,
    sol_hbm, res_hbm, dir_hbm, csol_hbm, cres_hbm, cdir_hbm,
    sol_buf, res_buf, dir_buf, csol_buf, cres_buf, cdir_buf, step_col, ratio_col, core_sems, sems,
):
    core = lax.axis_index("core")
    tile = sums_ref[0]
    for k in range(1, 16):
        tile = tile + sums_ref[k]
    tile = tile[:, 0:MEM]
    before = tile[0:1]
    step = before / tile[1:2]
    ratio = (before + step * (step * tile[3:4] - 2.0 * tile[2:3])) / before
    for j in range(NJ):
        csol_buf[j] = csol_ref[j] + step * cdir_ref[j]
        new_res = cres_ref[j] - step * cimage_ref[j]
        cres_buf[j] = new_res
        cdir_buf[j] = new_res + ratio * cdir_ref[j]
    waits = out_copies(
        [(csol_buf, csol_hbm), (cres_buf, cres_hbm), (cdir_buf, cdir_hbm)], core_sems
    )
    blank = jnp.zeros((1, 128 - MEM), F32)
    step_col[...] = turned(jnp.concatenate([step, blank], axis=1))
    ratio_col[...] = turned(jnp.concatenate([ratio, blank], axis=1))
    lane = lax.broadcasted_iota(jnp.int32, (8, SEG), 1)
    for y in range(5):
        cols = slice(y * FULL, min((y + 1) * FULL, NL))
        count = (cols.stop - cols.start) // SEG
        for k in range(8):
            ref, part = (own_ref, core) if k < 4 else (got_ref, 1 - core)
            rows = pl.ds(pl.multiple_of(part * 32 + (k % 4) * 8, 8), 8)
            if y < 4:
                image = ref[k % 4, y, :, 0:FULL]
            else:
                tails = [ref[k % 4, t, :, FULL:] for t in range(4)]
                image = jnp.concatenate(
                    [jnp.where(lane < HALF, tails[t], tails[t + 1]) for t in (0, 2)], axis=1
                )
            scale = jnp.concatenate([step_col[rows, :]] * count, axis=1)
            other = jnp.concatenate([ratio_col[rows, :]] * count, axis=1)
            direction = dir_ref[rows, cols]
            sol_buf[rows, cols] = sol_ref[rows, cols] + scale * direction
            new_res = res_ref[rows, cols] - scale * image
            res_buf[rows, cols] = new_res
            dir_buf[rows, cols] = new_res + other * direction
        waits += out_copies(
            [
                (buf.at[:, cols], hbm.at[:, cols])
                for buf, hbm in ((sol_buf, sol_hbm), (res_buf, res_hbm), (dir_buf, dir_hbm))
            ],
            sems.at[y],
        )
    for copy in waits:
        copy.wait()


def shards(
    design_lith, design_core, sample_phase, data_weight, counts, knot_index, lith_damping, core_damping,
    lith_solution, lith_residual, lith_direction, core_solution, core_residual, core_direction,
):
    segments = ("plane", "core")
    tm = lax.axis_size("plane") * 2
    swap = [(0, 1), (1, 0)]
    csol, cres, cdir = (
        jnp.transpose(v, (1, 2, 0)) for v in (core_solution, core_residual, core_direction)
    )
    phase = sample_phase.reshape(8, SEG)
    weight = data_weight.reshape(8, SEG)
    damp = lith_damping.reshape(NL // SEG, SEG)
    upper = lax.ppermute(cdir, segments, [(t, (t - 1) % tm) for t in range(tm)])
    product_cost = pl.CostEstimate(
        flops=16 * MEM * NL * NS, bytes_accessed=12 * MIB, transcendentals=0
    )

    pin = lambda v: pltpu.with_memory_space_constraint(v, pltpu.HBM)
    lith, design, ghi, glo = pl.pallas_call(
        forward_kernel,
        out_shape=(
            struct((MEM, NS)),
            pltpu.VMEM((NL, NS), BF16),
            struct((JP * 16, NS), BF16),
            struct((JP * 16, NS), BF16),
        ),
        in_specs=[HB, HB, VM, HB, HB, HB],
        out_specs=(VM,) * 4,
        scratch_shapes=[
            pltpu.VMEM((MEM, NL), F32),
            pltpu.VMEM((2 * MEM, NL), BF16),
            pltpu.VMEM((2 * MEM, NS), F32),
            pltpu.VMEM((8, SEG), F32),
            pltpu.SMEM((8,), jnp.int32),
            pltpu.VMEM((JP, 8, MEM), F32),
            pltpu.VMEM((16, NS), F32),
            pltpu.VMEM((JP, NS), F32),
            pltpu.SemaphoreType.DMA((4,)),
            pltpu.SemaphoreType.DMA((len(FORWARD_CUTS) - 1,)),
        ],
        compiler_params=params(24),
        cost_estimate=product_cost,
        name="forward",
    )(pin(lith_direction), pin(design_lith), design_core, pin(phase), pin(knot_index), pin(cdir))

    partial = pl.pallas_call(
        core_forward_kernel,
        out_shape=struct((8, 8, NS)),
        in_specs=[VM] * 4,
        out_specs=VM,
        scratch_shapes=[pltpu.VMEM((JP, 8, MEM), F32)],
        compiler_params=params(12),
        name="core_forward",
    )(lith, upper, ghi, glo)

    parts = lax.all_to_all(partial, "coef", 0, 0)
    total = pl.pallas_call(
        sum_kernel,
        out_shape=struct(parts.shape),
        in_specs=[VM],
        out_specs=VM,
        compiler_params=params(8),
        name="field_sum",
    )(parts)
    field = lax.all_to_all(total, "coef", 0, 0)

    chunks = struct((4, 4, 8, WIDE))
    core_struct = struct((NJ, 8, MEM))
    own, other, local, halo, curve = pl.pallas_call(
        back_kernel,
        out_shape=(chunks, chunks, core_struct, struct((HALO, 128)), struct((MEM, SEG))),
        in_specs=[VM] * 5 + [SM],
        out_specs=(VM,) * 5,
        scratch_shapes=[pltpu.VMEM((2 * MEM, NS), BF16), pltpu.VMEM((2 * MEM, NS), BF16)],
        compiler_params=params(16),
        cost_estimate=product_cost,
        name="back",
    )(field, weight, ghi, glo, design, counts)
    lower = lax.ppermute(halo, segments, [(t, (t + 1) % tm) for t in range(tm)])
    got = lax.ppermute(other, "core", swap)
    known = pl.pallas_call(
        known_sums_kernel,
        out_shape=struct((8, 128)),
        in_specs=[VM] * 5 + [SM],
        out_specs=VM,
        compiler_params=params(8),
        name="known_sums",
    )(cdir, cres, lith_direction, lith_residual, damp, core_damping)

    terms, known, cimage = pl.pallas_call(
        add_kernel,
        out_shape=(chunks, struct((8, 128)), core_struct),
        in_specs=[VM] * 7 + [SM],
        out_specs=(VM,) * 3,
        compiler_params=params(8),
        name="add_halves",
    )(own, got, known, local, lower, cdir, cres, core_damping)

    pieces = lax.all_to_all(terms.reshape(16, 8, WIDE), "plane", 0, 0)
    sent = pl.pallas_call(
        image_kernel,
        out_shape=struct((16, 8, WIDE)),
        in_specs=[VM] * 6,
        out_specs=VM,
        scratch_shapes=[pltpu.VMEM((8, WIDE), F32), pltpu.VMEM((2, MEM, 128), F32)],
        compiler_params=params(12),
        name="image",
    )(pieces, curve, lith_direction, lith_residual, damp, known)
    whole = lax.all_to_all(sent, "plane", 0, 0)
    rest = lax.ppermute(whole, "core", swap).reshape(4, 4, 8, WIDE)
    sums = pl.pallas_call(
        plane_sum_kernel,
        grid=(1,),
        out_shape=struct((16, 8, 128)),
        in_specs=[pl.BlockSpec((16, 8, 128), lambda i: (0, 0, FULL // 128))],
        out_specs=pl.BlockSpec((16, 8, 128), lambda i: (0, 0, 0)),
        compiler_params=params(8),
        name="plane_sum",
    )(whole)
    sums = lax.all_to_all(sums, ("core", "coef"), 0, 0)
    whole = whole.reshape(4, 4, 8, WIDE)

    lith_struct = struct((MEM, NL))
    new_sol, new_res, new_dir, new_csol, new_cres, new_cdir = pl.pallas_call(
        update_kernel,
        out_shape=(lith_struct,) * 3 + (core_struct,) * 3,
        in_specs=[VM] * 10,
        out_specs=(HB,) * 6,
        scratch_shapes=[pltpu.VMEM((MEM, NL), F32)] * 3
        + [pltpu.VMEM((NJ, 8, MEM), F32)] * 3
        + [pltpu.VMEM((128, 128), F32)] * 2
        + [pltpu.SemaphoreType.DMA((3,)), pltpu.SemaphoreType.DMA((5, 3))],
        compiler_params=params(20),
        name="update",
    )(
        whole, rest, sums, lith_solution, lith_residual, lith_direction, cimage, csol, cres, cdir,
    )
    first = lambda v: jnp.transpose(v, (2, 0, 1))
    return new_sol, new_res, new_dir, first(new_csol), first(new_cres), first(new_cdir)


def solution(mesh):
    parts = jax.sharding.Mesh(mesh.devices.reshape(-1, 2, mesh.devices.shape[1]), ("plane", "core", "coef"))
    segments = ("plane", "core")
    lith, core = P(None, "coef"), P(None, "coef", segments)
    return jax.shard_map(
        shards,
        mesh=parts,
        in_specs=(
            P("coef", segments), P("coef", segments), P(segments), P(segments), P(segments), P(segments),
            P("coef"), P("coef"), lith, lith, lith, core, core, core,
        ),
        out_specs=(lith, lith, lith, core, core, core),
        check_vma=False,
    )
```

```python
import jax
import jax.numpy as jnp
from jax import lax
from jax.experimental import pallas as pl
from jax.experimental.pallas import tpu as pltpu
from jax.sharding import PartitionSpec as P

NL, NS, MEM, NJ, JP = 4352, 1024, 64, 55, 56
GROWS = JP * 8
SEG = 128
WIDE, FULL, HALF, HALO = 1152, 1024, 64, 144
MIB = 1 << 20
F32, BF16 = jnp.float32, jnp.bfloat16
VM = pl.BlockSpec(memory_space=pltpu.VMEM)
SM = pl.BlockSpec(memory_space=pltpu.SMEM)
HB = pl.BlockSpec(memory_space=pltpu.HBM)
FORWARD_CUTS = (0, 768, 1792, 2816, 3840, 4352)
TRANS_B = (((1,), (1,)), ((), ()))


def params(mib):
    return pltpu.CompilerParams(vmem_limit_bytes=mib * MIB)


def struct(shape, dtype=F32):
    return jax.ShapeDtypeStruct(shape, dtype)


def split(values):
    high = values.astype(BF16)
    return high, (values - high.astype(F32)).astype(BF16)


def spline_values(u):
    now = [jnp.ones_like(u)]
    for d in range(1, 6):
        later = []
        for s in range(d + 1):
            term = 0.0
            if s >= 1:
                term = (u + float(d - s)) * now[s - 1]
            if s < d:
                term = term + (float(s + 1) - u) * now[s]
            later.append(term * (1.0 / d))
        now = later
    return now


def core_product(ext, ghi_ref, glo_ref, first):
    high, low = split(jnp.transpose(ext[...].reshape(GROWS, MEM)))
    both = jnp.concatenate([high, low], axis=0)
    rows = slice(first, first + GROWS)
    wide = jnp.dot(both, ghi_ref[rows, :], preferred_element_type=F32)
    low = jnp.dot(high, glo_ref[rows, :], preferred_element_type=F32)
    return wide[0:MEM] + wide[MEM:] + low


def forward_kernel(
    dir_hbm, a_hbm, design_ref, phase_hbm, knot_hbm, cdir_hbm, out_ref, a_buf, ghi_ref, glo_ref,
    dir_buf, lhs, acc, phase_buf, knot_buf, ext, basis, design, small_sems, sems,
):
    small = [
        pltpu.make_async_copy(src, dst, small_sems.at[k])
        for k, (src, dst) in enumerate(
            (
                (phase_hbm, phase_buf), (knot_hbm, knot_buf),
                (cdir_hbm, ext.at[0:NJ]), (dir_hbm, dir_buf),
            )
        )
    ]
    for copy in small:
        copy.start()
    copies = []
    for b in range(len(FORWARD_CUTS) - 1):
        rows = pl.ds(FORWARD_CUTS[b], FORWARD_CUTS[b + 1] - FORWARD_CUTS[b])
        copy = pltpu.make_async_copy(a_hbm.at[rows], a_buf.at[rows], sems.at[b])
        copy.start()
        copies.append(copy)
    for copy in small[0:3]:
        copy.wait()
    values = spline_values(phase_buf[...])
    row = lax.broadcasted_iota(jnp.int32, (16, SEG), 0)
    for g in range(8):
        first = lax.rem(knot_buf[g], 8)
        block = jnp.zeros((16, SEG), F32)
        for k in range(6):
            block = block + jnp.where(row == first + k, values[k][g : g + 1, :], 0.0)
        basis[:, g * SEG : (g + 1) * SEG] = block
    design[0:NJ] = design_ref[...].astype(F32)
    design[NJ:JP] = jnp.zeros((1, NS), F32)

    def build(j, carry):
        for part in range(2):
            spline = basis[part * 8 : part * 8 + 8, :]
            product = jnp.concatenate(
                [spline * design[pl.ds(2 * j + k, 1), :] for k in range(2)], axis=0
            )
            high, low = split(product)
            rows = pl.ds(pl.multiple_of(part * GROWS + j * 16, 16), 16)
            ghi_ref[rows, :] = high
            glo_ref[rows, :] = low
        return carry

    lax.fori_loop(0, JP // 2, build, 0)
    ext[NJ:JP] = jnp.zeros((1, 8, MEM), F32)
    out_ref[...] = core_product(ext, ghi_ref, glo_ref, 0)
    small[3].wait()
    for b, copy in enumerate(copies):
        lo, hi = FORWARD_CUTS[b], FORWARD_CUTS[b + 1]
        high, low = split(dir_buf[:, lo:hi])
        lhs[0:MEM, lo:hi] = high
        lhs[MEM:, lo:hi] = low
        copy.wait()
        part = jnp.dot(lhs[:, lo:hi], a_buf[lo:hi], preferred_element_type=F32)
        if b == 0:
            acc[...] = part
        else:
            acc[...] += part
    out_ref[...] += acc[0:MEM] + acc[MEM:]


def core_forward_kernel(lith_ref, halo_ref, ghi_ref, glo_ref, out_ref, ext):
    last = jnp.logical_and(lax.axis_index("plane") == 15, lax.axis_index("core") == 1)
    ext[0:NJ] = halo_ref[...] * jnp.where(last, 0.0, 1.0)
    ext[NJ:JP] = jnp.zeros((1, 8, MEM), F32)
    value = core_product(ext, ghi_ref, glo_ref, GROWS) + lith_ref[...]
    out_ref[...] = value.reshape(8, 8, NS)


def sum_kernel(parts_ref, out_ref):
    total = parts_ref[0]
    for k in range(1, parts_ref.shape[0]):
        total = total + parts_ref[k]
    for k in range(parts_ref.shape[0]):
        out_ref[k] = total


def back_kernel(
    field_ref, weight_ref, ghi_ref, glo_ref, a_ref, count_ref,
    own_ref, other_ref, local_ref, halo_ref, curve_ref, pair, lhs,
):
    lane = lax.broadcasted_iota(jnp.int32, (1, SEG), 1)
    curve = jnp.zeros((MEM, SEG), F32)
    for g in range(8):
        cols = slice(g * SEG, (g + 1) * SEG)
        weight = jnp.where(lane < count_ref[g], weight_ref[g : g + 1, :], 0.0)
        field = field_ref[:, :, cols].reshape(MEM, SEG)
        residual = field * weight
        curve = curve + residual * field
        high, low = split(residual)
        pair[0:MEM, cols] = high
        pair[MEM:, cols] = low
    curve_ref[...] = curve
    half = MEM // 2
    core = lax.axis_index("core")
    mine = pl.multiple_of(core * half, half)
    theirs = pl.multiple_of((1 - core) * half, half)
    for k, start in enumerate((mine, theirs, MEM + mine, MEM + theirs)):
        lhs[k * half : (k + 1) * half] = pair[pl.ds(pl.multiple_of(start, half), half), :]

    def product(rows):
        part = lax.dot_general(lhs[...], a_ref[rows], TRANS_B, preferred_element_type=F32)
        part = part[0:MEM] + part[MEM:]
        return part[0:half], part[half:]

    for y in range(4):
        for out, part in zip((own_ref, other_ref), product(slice(y * FULL, (y + 1) * FULL))):
            out[:, y, :, 0:FULL] = part.reshape(4, 8, FULL)
    for out, part in zip((own_ref, other_ref), product(slice(4 * FULL, NL))):
        for y in range(4):
            tail = part[:, y // 2 * SEG : (y // 2 + 1) * SEG]
            out[:, y, :, FULL:] = tail.reshape(4, 8, SEG)
    wide = lax.dot_general(ghi_ref[...], pair[...], TRANS_B, preferred_element_type=F32)
    low = lax.dot_general(glo_ref[...], pair[0:MEM], TRANS_B, preferred_element_type=F32)
    grad = (wide[:, 0:MEM] + wide[:, MEM:] + low).reshape(2, JP, 8, MEM)
    local_ref[...] = grad[0, 0:NJ]
    packed = jnp.concatenate([grad[1, 0 : JP // 2], grad[1, JP // 2 :]], axis=2)
    for j in range(JP // 2):
        halo_ref[j * 5 : j * 5 + 5, :] = packed[j, 0:5, :]
    halo_ref[JP // 2 * 5 :, :] = jnp.zeros((HALO - JP // 2 * 5, 128), F32)


def add_kernel(
    own_ref, got_ref, tile_ref, local_ref, halo_ref, cdir_ref, cres_ref, cdamp_ref,
    out_ref, tile_out_ref, cimage_ref,
):
    out_ref[...] = own_ref[...] + got_ref[...]
    cross = jnp.zeros((8, MEM), F32)
    norm = jnp.zeros((8, MEM), F32)
    first = jnp.logical_and(lax.axis_index("plane") == 0, lax.axis_index("core") == 0)
    row = lax.broadcasted_iota(jnp.int32, (8, 128), 0)
    inside = jnp.where(row < 5, jnp.where(first, 0.0, 1.0), 0.0)
    for j in range(NJ):
        place = j % (JP // 2) * 5
        packed = halo_ref[place : place + 8, :] * inside
        halo = packed[:, 0:MEM] if j < JP // 2 else packed[:, MEM:]
        core_image = local_ref[j] + halo + cdamp_ref[j] * cdir_ref[j]
        cimage_ref[j] = core_image
        cross = cross + cres_ref[j] * core_image
        norm = norm + core_image * core_image
    zero = jnp.zeros((1, MEM), F32)
    tile_out_ref[...] = tile_ref[...] + tile_of(
        [zero, zero, jnp.sum(cross, axis=0, keepdims=True), jnp.sum(norm, axis=0, keepdims=True)]
    )


def turned(row):
    return jnp.transpose(jnp.broadcast_to(row, (128, 128)))


def out_copies(pairs, sems):
    copies = [
        pltpu.make_async_copy(src, dst, sems.at[k]) for k, (src, dst) in enumerate(pairs)
    ]
    for copy in copies:
        copy.start()
    return copies


def damp_rows(damp_ref, cols):
    rows = range(cols.start // SEG, cols.stop // SEG)
    return jnp.concatenate(
        [jnp.broadcast_to(damp_ref[t : t + 1, :], (8, SEG)) for t in rows], axis=1
    )


def folded(values):
    total = values[:, 0:SEG]
    for t in range(1, values.shape[1] // SEG):
        total = total + values[:, t * SEG : (t + 1) * SEG]
    return total


def member_row(columns):
    padded = jnp.concatenate([columns, jnp.zeros((128 - MEM, 128), F32)], axis=0)
    return jnp.sum(jnp.transpose(padded), axis=0, keepdims=True)[:, 0:MEM]


def tile_of(rows):
    tile = jnp.concatenate(rows + [jnp.zeros((8 - len(rows), MEM), F32)], axis=0)
    return jnp.concatenate([tile, jnp.zeros((8, 128 - MEM), F32)], axis=1)


def known_sums_kernel(cdir_ref, cres_ref, dir_ref, res_ref, damp_ref, cdamp_ref, tile_ref):
    before = jnp.zeros((8, MEM), F32)
    curve = jnp.zeros((8, MEM), F32)
    for j in range(NJ):
        before = before + cres_ref[j] * cres_ref[j]
        curve = curve + cdamp_ref[j] * (cdir_ref[j] * cdir_ref[j])
    lith_before = jnp.zeros((MEM, SEG), F32)
    lith_curve = jnp.zeros((MEM, SEG), F32)
    for t in range(NL // SEG):
        cols = slice(t * SEG, (t + 1) * SEG)
        lith_before = lith_before + res_ref[:, cols] * res_ref[:, cols]
        lith_curve = lith_curve + dir_ref[:, cols] * dir_ref[:, cols] * damp_ref[t : t + 1, :]
    once = jnp.logical_and(lax.axis_index("plane") == 0, lax.axis_index("core") == 0)
    once = jnp.where(once, 1.0, 0.0)
    tile_ref[...] = tile_of(
        [
            jnp.sum(c, axis=0, keepdims=True) + once * member_row(v)
            for c, v in ((before, lith_before), (curve, lith_curve))
        ]
    )


def image_kernel(parts_ref, curve_ref, dir_ref, res_ref, damp_ref, tile_ref, out_ref, image, square):
    total = parts_ref[0]
    for k in range(1, 16):
        total = total + parts_ref[k]
    image[...] = total
    square[...] = jnp.zeros((2, MEM, 128), F32)
    plane = lax.axis_index("plane")
    rows = pl.ds(pl.multiple_of((lax.axis_index("core") * 4 + plane // 4) * 8, 8), 8)
    lane = lax.broadcasted_iota(jnp.int32, (8, SEG), 1)
    mine = lane // HALF == lax.rem(plane, 2)

    def finish(y):
        cols = slice(y * FULL, (y + 1) * FULL)
        tail = slice(4 * FULL + y // 2 * SEG, 4 * FULL + (y // 2 + 1) * SEG)
        value = image[:, 0:FULL] + damp_rows(damp_ref, cols) * dir_ref[rows, cols]
        rest = image[:, FULL:] + damp_rows(damp_ref, tail) * dir_ref[rows, tail]
        rest = jnp.where(mine, rest, 0.0)
        image[:, 0:FULL] = value
        image[:, FULL:] = rest
        square[0, rows, :] = folded(value * res_ref[rows, cols]) + rest * res_ref[rows, tail]
        square[1, rows, :] = folded(value * value) + rest * rest

    for y in range(4):
        pl.when(lax.rem(plane, 4) == y)(lambda y=y: finish(y))
    first = jnp.where(lax.axis_index("coef") == 0, 1.0, 0.0)
    tile = tile_ref[...] + tile_of(
        [
            jnp.zeros((1, MEM), F32),
            first * member_row(curve_ref[...]),
            member_row(square[0]),
            member_row(square[1]),
        ]
    )
    tile = jnp.concatenate([tile[:, 0:HALF], tile[:, 0:HALF]], axis=1)
    rest = jnp.where(mine, image[:, FULL:], tile)
    for k in range(16):
        out_ref[k, :, 0:FULL] = image[:, 0:FULL]
        out_ref[k, :, FULL:] = rest


def plane_sum_kernel(whole_ref, out_ref):
    even, odd = whole_ref[0], whole_ref[1]
    for k in range(2, 16, 2):
        even = even + whole_ref[k]
        odd = odd + whole_ref[k + 1]
    tile = odd[:, 0:HALF] + even[:, HALF:]
    tile = jnp.concatenate([tile, jnp.zeros((8, SEG - HALF), F32)], axis=1)
    for k in range(16):
        out_ref[k] = tile


def update_kernel(
    own_ref, got_ref, sums_ref, sol_ref, res_ref, dir_ref, cimage_ref, csol_ref, cres_ref, cdir_ref,
    sol_hbm, res_hbm, dir_hbm, csol_hbm, cres_hbm, cdir_hbm,
    sol_buf, res_buf, dir_buf, csol_buf, cres_buf, cdir_buf, step_col, ratio_col, core_sems, sems,
):
    core = lax.axis_index("core")
    tile = sums_ref[0]
    for k in range(1, 16):
        tile = tile + sums_ref[k]
    tile = tile[:, 0:MEM]
    before = tile[0:1]
    step = before / tile[1:2]
    ratio = (before + step * (step * tile[3:4] - 2.0 * tile[2:3])) / before
    for j in range(NJ):
        csol_buf[j] = csol_ref[j] + step * cdir_ref[j]
        new_res = cres_ref[j] - step * cimage_ref[j]
        cres_buf[j] = new_res
        cdir_buf[j] = new_res + ratio * cdir_ref[j]
    waits = out_copies(
        [(csol_buf, csol_hbm), (cres_buf, cres_hbm), (cdir_buf, cdir_hbm)], core_sems
    )
    blank = jnp.zeros((1, 128 - MEM), F32)
    step_col[...] = turned(jnp.concatenate([step, blank], axis=1))
    ratio_col[...] = turned(jnp.concatenate([ratio, blank], axis=1))
    lane = lax.broadcasted_iota(jnp.int32, (8, SEG), 1)
    for y in range(5):
        cols = slice(y * FULL, min((y + 1) * FULL, NL))
        count = (cols.stop - cols.start) // SEG
        for k in range(8):
            ref, part = (own_ref, core) if k < 4 else (got_ref, 1 - core)
            rows = pl.ds(pl.multiple_of(part * 32 + (k % 4) * 8, 8), 8)
            if y < 4:
                image = ref[k % 4, y, :, 0:FULL]
            else:
                tails = [ref[k % 4, t, :, FULL:] for t in range(4)]
                image = jnp.concatenate(
                    [jnp.where(lane < HALF, tails[t], tails[t + 1]) for t in (0, 2)], axis=1
                )
            scale = jnp.concatenate([step_col[rows, :]] * count, axis=1)
            other = jnp.concatenate([ratio_col[rows, :]] * count, axis=1)
            direction = dir_ref[rows, cols]
            sol_buf[rows, cols] = sol_ref[rows, cols] + scale * direction
            new_res = res_ref[rows, cols] - scale * image
            res_buf[rows, cols] = new_res
            dir_buf[rows, cols] = new_res + other * direction
        waits += out_copies(
            [
                (buf.at[:, cols], hbm.at[:, cols])
                for buf, hbm in ((sol_buf, sol_hbm), (res_buf, res_hbm), (dir_buf, dir_hbm))
            ],
            sems.at[y],
        )
    for copy in waits:
        copy.wait()


def shards(
    design_lith, design_core, sample_phase, data_weight, counts, knot_index, lith_damping, core_damping,
    lith_solution, lith_residual, lith_direction, core_solution, core_residual, core_direction,
):
    segments = ("plane", "core")
    tm = lax.axis_size("plane") * 2
    swap = [(0, 1), (1, 0)]
    csol, cres, cdir = (
        jnp.transpose(v, (1, 2, 0)) for v in (core_solution, core_residual, core_direction)
    )
    phase = sample_phase.reshape(8, SEG)
    weight = data_weight.reshape(8, SEG)
    damp = lith_damping.reshape(NL // SEG, SEG)
    upper = lax.ppermute(cdir, segments, [(t, (t - 1) % tm) for t in range(tm)])
    product_cost = pl.CostEstimate(
        flops=16 * MEM * NL * NS, bytes_accessed=12 * MIB, transcendentals=0
    )

    pin = lambda v: pltpu.with_memory_space_constraint(v, pltpu.HBM)
    lith, design, ghi, glo = pl.pallas_call(
        forward_kernel,
        out_shape=(
            struct((MEM, NS)),
            pltpu.VMEM((NL, NS), BF16),
            struct((JP * 16, NS), BF16),
            struct((JP * 16, NS), BF16),
        ),
        in_specs=[HB, HB, VM, HB, HB, HB],
        out_specs=(VM,) * 4,
        scratch_shapes=[
            pltpu.VMEM((MEM, NL), F32),
            pltpu.VMEM((2 * MEM, NL), BF16),
            pltpu.VMEM((2 * MEM, NS), F32),
            pltpu.VMEM((8, SEG), F32),
            pltpu.SMEM((8,), jnp.int32),
            pltpu.VMEM((JP, 8, MEM), F32),
            pltpu.VMEM((16, NS), F32),
            pltpu.VMEM((JP, NS), F32),
            pltpu.SemaphoreType.DMA((4,)),
            pltpu.SemaphoreType.DMA((len(FORWARD_CUTS) - 1,)),
        ],
        compiler_params=params(24),
        cost_estimate=product_cost,
        name="forward",
    )(pin(lith_direction), pin(design_lith), design_core, pin(phase), pin(knot_index), pin(cdir))

    partial = pl.pallas_call(
        core_forward_kernel,
        out_shape=struct((8, 8, NS)),
        in_specs=[VM] * 4,
        out_specs=VM,
        scratch_shapes=[pltpu.VMEM((JP, 8, MEM), F32)],
        compiler_params=params(12),
        name="core_forward",
    )(lith, upper, ghi, glo)

    parts = lax.all_to_all(partial, "coef", 0, 0)
    total = pl.pallas_call(
        sum_kernel,
        out_shape=struct(parts.shape),
        in_specs=[VM],
        out_specs=VM,
        compiler_params=params(8),
        name="field_sum",
    )(parts)
    field = lax.all_to_all(total, "coef", 0, 0)

    chunks = struct((4, 4, 8, WIDE))
    core_struct = struct((NJ, 8, MEM))
    own, other, local, halo, curve = pl.pallas_call(
        back_kernel,
        out_shape=(chunks, chunks, core_struct, struct((HALO, 128)), struct((MEM, SEG))),
        in_specs=[VM] * 5 + [SM],
        out_specs=(VM,) * 5,
        scratch_shapes=[pltpu.VMEM((2 * MEM, NS), BF16), pltpu.VMEM((2 * MEM, NS), BF16)],
        compiler_params=params(16),
        cost_estimate=product_cost,
        name="back",
    )(field, weight, ghi, glo, design, counts)
    lower = lax.ppermute(halo, segments, [(t, (t + 1) % tm) for t in range(tm)])
    got = lax.ppermute(other, "core", swap)
    known = pl.pallas_call(
        known_sums_kernel,
        out_shape=struct((8, 128)),
        in_specs=[VM] * 5 + [SM],
        out_specs=VM,
        compiler_params=params(8),
        name="known_sums",
    )(cdir, cres, lith_direction, lith_residual, damp, core_damping)

    terms, known, cimage = pl.pallas_call(
        add_kernel,
        out_shape=(chunks, struct((8, 128)), core_struct),
        in_specs=[VM] * 7 + [SM],
        out_specs=(VM,) * 3,
        compiler_params=params(8),
        name="add_halves",
    )(own, got, known, local, lower, cdir, cres, core_damping)

    pieces = lax.all_to_all(terms.reshape(16, 8, WIDE), "plane", 0, 0)
    sent = pl.pallas_call(
        image_kernel,
        out_shape=struct((16, 8, WIDE)),
        in_specs=[VM] * 6,
        out_specs=VM,
        scratch_shapes=[pltpu.VMEM((8, WIDE), F32), pltpu.VMEM((2, MEM, 128), F32)],
        compiler_params=params(12),
        name="image",
    )(pieces, curve, lith_direction, lith_residual, damp, known)
    whole = lax.all_to_all(sent, "plane", 0, 0)
    rest = lax.ppermute(whole, "core", swap).reshape(4, 4, 8, WIDE)
    sums = pl.pallas_call(
        plane_sum_kernel,
        grid=(1,),
        out_shape=struct((16, 8, 128)),
        in_specs=[pl.BlockSpec((16, 8, 128), lambda i: (0, 0, FULL // 128))],
        out_specs=pl.BlockSpec((16, 8, 128), lambda i: (0, 0, 0)),
        compiler_params=params(8),
        name="plane_sum",
    )(whole)
    sums = lax.all_to_all(sums, ("core", "coef"), 0, 0)
    whole = whole.reshape(4, 4, 8, WIDE)

    lith_struct = struct((MEM, NL))
    new_sol, new_res, new_dir, new_csol, new_cres, new_cdir = pl.pallas_call(
        update_kernel,
        out_shape=(lith_struct,) * 3 + (core_struct,) * 3,
        in_specs=[VM] * 10,
        out_specs=(HB,) * 6,
        scratch_shapes=[pltpu.VMEM((MEM, NL), F32)] * 3
        + [pltpu.VMEM((NJ, 8, MEM), F32)] * 3
        + [pltpu.VMEM((128, 128), F32)] * 2
        + [pltpu.SemaphoreType.DMA((3,)), pltpu.SemaphoreType.DMA((5, 3))],
        compiler_params=params(20),
        name="update",
    )(
        whole, rest, sums, lith_solution, lith_residual, lith_direction, cimage, csol, cres, cdir,
    )
    first = lambda v: jnp.transpose(v, (2, 0, 1))
    return new_sol, new_res, new_dir, first(new_csol), first(new_cres), first(new_cdir)


def solution(mesh):
    parts = jax.sharding.Mesh(mesh.devices.reshape(-1, 2, mesh.devices.shape[1]), ("plane", "core", "coef"))
    segments = ("plane", "core")
    lith, core = P(None, "coef"), P(None, "coef", segments)
    return jax.shard_map(
        shards,
        mesh=parts,
        in_specs=(
            P("coef", segments), P("coef", segments), P(segments), P(segments), P(segments), P(segments),
            P("coef"), P("coef"), lith, lith, lith, core, core, core,
        ),
        out_specs=(lith, lith, lith, core, core, core),
        check_vma=False,
    )
```
